32 devices in a mesh: row: 8 (over z, core), col: 4 (over y, x).
Axes of the slice: x: 2, y: 2, z: 4, core: 2. Of those that a mesh axis runs over, the one named last changes fastest.
Arguments:
- layer_input: bfloat16 [2048, 8192], P('row', 'col'), may hold values from -6 to 6
- attn_grad: bfloat16 [2048, 8192], P('row', 'col'), may hold values from -6 to 6
- queries: bfloat16 [8, 256, 8192], P('row', None, 'col'), may hold values from -6 to 6
- keys: bfloat16 [8, 256, 8192], P('row', None, 'col'), may hold values from -6 to 6
- values: bfloat16 [8, 256, 8192], P('row', None, 'col'), may hold values from -6 to 6
- masked: int32 [8, 256], P('row'), may hold values 0 or 1
- key_bias: float32 [64], P('col'), may hold values from -2 to 2
- w_query: bfloat16 [8192, 8192], P('row', 'col'), may hold values from -0.0625 to 0.0625
- w_key: bfloat16 [8192, 8192], P('row', 'col'), may hold values from -0.0625 to 0.0625
- w_value: bfloat16 [8192, 8192], P('row', 'col'), may hold values from -0.0625 to 0.0625
Outputs:
- layer_grad: bfloat16 [2048, 8192], P('row', 'col')
- w_query_grad: bfloat16 [8192, 8192], P('row', 'col')
- w_key_grad: bfloat16 [8192, 8192], P('row', 'col')
- w_value_grad: bfloat16 [8192, 8192], P('row', 'col')
- bias_grad: float32 [64], P('col')
The draws below stay inside these ranges and needn't reach their ends.
All inputs are finite; a program needn't handle non-finite values. No bound on the sum of `masked` on one device may be relied on, other than what follows from the above.
Results may differ from the reference program's by a relative error of at most 0.015.
Values may be sent and summed in bfloat16 or wider, within the bound.
No kernel may reach another device: no remote copies, remote signals or barrier semaphores. Data moves between devices by JAX's collectives and lax.ppermute only.
A program may use at most 192 MiB of HBM per device.

```python
import jax
import jax.numpy as jnp
from jax import lax

D = 8192
HEADS = 64
SEQ = 256
HD = 128
CANV = 8
TOKENS = 2048
N_COL = 4


def shared_draw(key):
    folded = jax.random.fold_in(key, 7101)
    key_query, key_keys = jax.random.split(folded, 2)
    head_dim = D // HEADS
    grid_shape = (CANV, SEQ, HEADS, head_dim)
    query_vals = jnp.clip(jax.random.normal(key_query, grid_shape, jnp.float32), -4.5, 4.5)
    key_vals = jnp.clip(jax.random.normal(key_keys, grid_shape, jnp.float32), -4.5, 4.5)
    return (query_vals.reshape(CANV, SEQ, D), key_vals.reshape(CANV, SEQ, D))


def draw_queries(key, part):
    return shared_draw(key)[0].astype(jnp.bfloat16)


def draw_keys(key, part):
    return shared_draw(key)[1].astype(jnp.bfloat16)


def place_ends(array, rng, least, high):
    place = [jax.random.randint(jax.random.fold_in(rng, axis), (), 0, length) for axis, length in enumerate(array.shape)]
    widest = array.shape.index(max(array.shape))
    next_to = place[:widest] + [(place[widest] + 1) % array.shape[widest]] + place[widest + 1:]
    return array.at[tuple(place)].set(least).at[tuple(next_to)].set(high)


def shard_levels(rng, extent, shards, least, high):
    gain = 1.0
    for position, shards_of in shards:
        draws = jax.random.uniform(jax.random.fold_in(jax.random.fold_in(rng, 6), position), (shards_of,), jnp.float32, least / len(shards), high / len(shards))
        gain = gain * jnp.repeat(jnp.exp(draws), extent[position] // shards_of).reshape((-1,) + (1,) * (len(extent) - 1 - position))
    return gain


def normal_values(own_key, extent, spread, limit, cuts=(), dtype=jnp.bfloat16):
    gain = shard_levels(own_key, extent, cuts, -0.22, 0.18) if cuts else 1.0
    entries = jax.random.normal(own_key, extent, jnp.float32) * spread * gain
    return jnp.minimum(jnp.maximum(entries, -limit), limit).astype(dtype)


def setup_inputs(seed: int = 0) -> dict:
    streams_of = jax.random.split(jax.random.key(seed), 11)
    return {
        "layer_input": normal_values(streams_of[0], (TOKENS, D), 1.0, 6.0, ((0, 8), (1, 4))),
        "attn_grad": normal_values(streams_of[1], (TOKENS, D), 1.0, 6.0, ((0, 8), (1, 4))),
        "queries": draw_queries(jax.random.fold_in(streams_of[10], 71), 0),
        "keys": draw_keys(jax.random.fold_in(streams_of[10], 71), 0),
        "values": normal_values(streams_of[4], (CANV, SEQ, D), 1.0, 6.0, ((0, 8), (2, 4))),
        "masked": place_ends((jax.random.randint(streams_of[5], (CANV, SEQ), 0, 2) < 1).astype(jnp.int32), jax.random.fold_in(streams_of[5], 1), 0, 1),
        "key_bias": jnp.clip(jax.random.uniform(streams_of[6], (HEADS,), jnp.float32, -2.0, 2.0) * shard_levels(streams_of[6], (HEADS,), ((0, 4),), -0.4, 0.0), -2.0, 2.0),
        "w_query": normal_values(streams_of[7], (D, D), D ** -0.5, 0.0625, ((0, 8), (1, 4))),
        "w_key": normal_values(streams_of[8], (D, D), D ** -0.5, 0.0625, ((0, 8), (1, 4))),
        "w_value": normal_values(streams_of[9], (D, D), D ** -0.5, 0.0625, ((0, 8), (1, 4))),
    }


def canvas_backward(query_c, key_c, value_c, grad_c, flag_c, key_bias):
    scale_qk = 1.0 / jnp.sqrt(jnp.float32(HD))
    query_h = query_c.reshape(SEQ, HEADS, HD).astype(jnp.float32)
    key_h = key_c.reshape(SEQ, HEADS, HD).astype(jnp.float32)
    value_h = value_c.reshape(SEQ, HEADS, HD).astype(jnp.float32)
    grad_h = grad_c.reshape(SEQ, HEADS, HD).astype(jnp.float32)
    flag_float = flag_c.astype(jnp.float32)
    scores = jnp.einsum('ihd,jhd->hij', query_h, key_h) * scale_qk + key_bias[:, None, None] * flag_float[None, None, :]
    row_max = lax.optimization_barrier(jnp.max(scores, axis=-1, keepdims=True))
    exp_terms = jnp.exp(scores - row_max)
    attn_probs = exp_terms / lax.optimization_barrier(jnp.sum(exp_terms, axis=-1, keepdims=True))
    probs_low = lax.optimization_barrier(attn_probs.astype(jnp.bfloat16)).astype(jnp.float32)
    attended = jnp.einsum('hij,jhd->ihd', probs_low, value_h)
    delta = lax.optimization_barrier(jnp.sum(grad_h * attended, axis=-1))
    grad_probs = jnp.einsum('ihd,jhd->hij', grad_h, value_h)
    grad_scores = attn_probs * (grad_probs - jnp.transpose(delta)[:, :, None])
    grad_low = lax.optimization_barrier(grad_scores.astype(jnp.bfloat16)).astype(jnp.float32)
    value_grad = jnp.einsum('hij,ihd->jhd', probs_low, grad_h).astype(jnp.bfloat16)
    query_grad = (jnp.einsum('hij,jhd->ihd', grad_low, key_h) * scale_qk).astype(jnp.bfloat16)
    key_grad = (jnp.einsum('hij,ihd->jhd', grad_low, query_h) * scale_qk).astype(jnp.bfloat16)
    bias_part = lax.optimization_barrier(jnp.sum(grad_scores * flag_float[None, None, :], axis=(1, 2)))
    return (query_grad.reshape(SEQ, D), key_grad.reshape(SEQ, D), value_grad.reshape(SEQ, D), bias_part)

def reference(layer_input, attn_grad, queries, keys, values, masked, key_bias, w_query, w_key, w_value):
    grad_canvas = attn_grad.reshape(CANV, SEQ, D)

    def one_canvas(inputs_one):
        return canvas_backward(inputs_one[0], inputs_one[1], inputs_one[2], inputs_one[3], inputs_one[4], key_bias)
    query_grad, key_grad, value_grad, bias_parts = lax.map(one_canvas, (queries, keys, values, grad_canvas, masked))
    bias_grad = lax.optimization_barrier(jnp.sum(bias_parts, axis=0))
    flat_grads = (query_grad.reshape(TOKENS, D), key_grad.reshape(TOKENS, D), value_grad.reshape(TOKENS, D))
    weights = (w_query, w_key, w_value)
    input_t = layer_input.T
    weight_grads = [jnp.dot(input_t, member, preferred_element_type=jnp.float32).astype(jnp.bfloat16) for member in flat_grads]
    width_col = D // N_COL
    accumulated = jnp.zeros((TOKENS, D), jnp.float32)
    for column in range(N_COL):
        col_start = column * width_col
        col_part = jnp.zeros((TOKENS, D), jnp.float32)
        for member, weight in zip(flat_grads, weights):
            col_part = col_part + jnp.dot(member[:, col_start:col_start + width_col], weight[:, col_start:col_start + width_col].T, preferred_element_type=jnp.float32)
        accumulated = accumulated + lax.optimization_barrier(col_part.astype(jnp.bfloat16)).astype(jnp.float32)
    layer_grad = accumulated.astype(jnp.bfloat16)
    return (layer_grad, weight_grads[0], weight_grads[1], weight_grads[2], bias_grad)
```

```python
import functools
import math

import jax
import jax.numpy as jnp
from jax import lax
from jax.experimental import pallas as pl
from jax.experimental.pallas import tpu as pltpu
from jax.sharding import PartitionSpec as P

NT = (((1,), (1,)), ((), ()))
TN = (((0,), (0,)), ((), ()))
VMEM_LIMIT = 56 * 1024 * 1024


def chunk_sizes(length):
    return (length // 2, length - length // 2)


def attention_body(sizes, head_dim, heads_step, bias_ref, flag_ref, q_ref, k_ref, v_ref, g_ref, *outs):
    chunk_refs, bias_out = outs[:-1], outs[-1]
    scale_qk = 1.0 / math.sqrt(head_dim)
    flag = flag_ref[...].astype(jnp.float32)
    for sub in range(heads_step):
        cols = slice(sub * head_dim, (sub + 1) * head_dim)
        q, k, v, g = q_ref[:, cols], k_ref[:, cols], v_ref[:, cols], g_ref[:, cols]
        head = pl.program_id(0) * heads_step + sub
        scores = lax.dot_general(q, k, NT, preferred_element_type=jnp.float32) * scale_qk + bias_ref[head] * flag
        exp_terms = jnp.exp(scores - jnp.max(scores, axis=-1, keepdims=True))
        probs = exp_terms * (1.0 / jnp.sum(exp_terms, axis=-1, keepdims=True))
        probs_low = probs.astype(jnp.bfloat16)
        grad_probs = lax.dot_general(g, v, NT, preferred_element_type=jnp.float32)
        delta = jnp.sum(probs_low.astype(jnp.float32) * grad_probs, axis=-1, keepdims=True)
        grad_scores = probs * (grad_probs - delta)
        grad_low = grad_scores.astype(jnp.bfloat16)
        value_grad = lax.dot_general(probs_low, g, TN, preferred_element_type=jnp.float32)
        query_grad = jnp.dot(grad_low, k, preferred_element_type=jnp.float32) * scale_qk
        key_grad = lax.dot_general(grad_low, q, TN, preferred_element_type=jnp.float32) * scale_qk
        bias = jnp.sum(jnp.sum(grad_scores, axis=0, keepdims=True) * flag, axis=1, keepdims=True)
        bias_out[sub] = jnp.broadcast_to(bias, (1, 128))
        for place, member in enumerate((query_grad, key_grad, value_grad)):
            low = member.astype(jnp.bfloat16)
            begin = 0
            for size, ref in zip(sizes, chunk_refs):
                ref[place, :, cols] = low[begin:begin + size]
                begin += size


def attention(queries, keys, values, grads, flags, key_bias, sizes):
    length, width = queries.shape
    heads = key_bias.shape[0]
    head_dim = width // heads
    heads_step = 2 if heads % 2 == 0 else 1
    block = pl.BlockSpec((length, heads_step * head_dim), lambda h: (0, h))
    outs = pl.pallas_call(
        functools.partial(attention_body, sizes, head_dim, heads_step),
        grid=(heads // heads_step,),
        in_specs=[
            pl.BlockSpec(memory_space=pltpu.SMEM),
            pl.BlockSpec((1, length), lambda h: (0, 0)),
            block, block, block, block,
        ],
        out_specs=[pl.BlockSpec((3, size, heads_step * head_dim), lambda h: (0, 0, h)) for size in sizes]
        + [pl.BlockSpec((heads_step, 1, 128), lambda h: (h, 0, 0))],
        out_shape=[jax.ShapeDtypeStruct((3, size, width), jnp.bfloat16) for size in sizes]
        + [jax.ShapeDtypeStruct((heads, 1, 128), jnp.float32)],
        compiler_params=pltpu.CompilerParams(vmem_limit_bytes=VMEM_LIMIT),
        cost_estimate=pl.CostEstimate(
            flops=10 * length * length * width, bytes_accessed=14 * length * width, transcendentals=heads * length * length
        ),
        name="attention_back",
    )(key_bias, flags, queries, keys, values, grads)
    return outs[:-1], outs[-1][:, 0, 0]


def input_grad_body(count, pieces, *refs):
    grad_refs, weight_refs, out_ref = refs[:count], refs[count:count + 3], refs[-1]
    total = None
    for member in range(3):
        rows = jnp.concatenate([ref[member] for ref in grad_refs], axis=0)
        term = lax.dot_general(rows, weight_refs[member][...], NT, preferred_element_type=jnp.float32)
        total = term if total is None else total + term
    low = total.astype(jnp.bfloat16)
    begin = 0
    at = 0
    for ref in grad_refs:
        size = ref.shape[1] // pieces
        for piece in range(pieces):
            out_ref[piece, at:at + size, :] = low[begin:begin + size]
            begin += size
        at += size


def input_grad(grads, weights, pieces):
    rows_in, width = weights[0].shape
    tokens = sum(grad.shape[1] for grad in grads)
    step = 256
    return pl.pallas_call(
        functools.partial(input_grad_body, len(grads), pieces),
        grid=(rows_in // step,),
        in_specs=[pl.BlockSpec(grad.shape, lambda n: (0, 0, 0)) for grad in grads]
        + [pl.BlockSpec((step, width), lambda n: (n, 0))] * 3,
        out_specs=pl.BlockSpec((pieces, tokens // pieces, step), lambda n: (0, 0, n)),
        out_shape=jax.ShapeDtypeStruct((pieces, tokens // pieces, rows_in), jnp.bfloat16),
        compiler_params=pltpu.CompilerParams(vmem_limit_bytes=VMEM_LIMIT),
        cost_estimate=pl.CostEstimate(
            flops=6 * tokens * rows_in * width, bytes_accessed=6 * width * (rows_in + tokens), transcendentals=0
        ),
        name="input_grad",
    )(*grads, *weights)


def weight_grad_body(count, has_acc, x_ref, *refs):
    grad_refs, out_refs = refs[:count], refs[-3:]
    for member in range(3):
        right = jnp.concatenate([ref[member] for ref in grad_refs], axis=0)
        total = jnp.dot(x_ref[...], right, preferred_element_type=jnp.float32)
        if has_acc:
            total = total + refs[count + member][...].astype(jnp.float32)
        out_refs[member][...] = total.astype(jnp.bfloat16)


def weight_grad(x_turned, grads, acc):
    rows_in, tokens = x_turned.shape
    width = grads[0].shape[2]
    step = 256
    block = pl.BlockSpec((rows_in, step), lambda n: (0, n))
    acc = tuple(acc) if acc is not None else ()
    return pl.pallas_call(
        functools.partial(weight_grad_body, len(grads), bool(acc)),
        grid=(width // step,),
        in_specs=[pl.BlockSpec((rows_in, tokens), lambda n: (0, 0))]
        + [pl.BlockSpec((3, grad.shape[1], step), lambda n: (0, 0, n)) for grad in grads]
        + [block] * len(acc),
        out_specs=[block] * 3,
        out_shape=[jax.ShapeDtypeStruct((rows_in, width), jnp.bfloat16)] * 3,
        compiler_params=pltpu.CompilerParams(vmem_limit_bytes=VMEM_LIMIT),
        cost_estimate=pl.CostEstimate(
            flops=6 * tokens * rows_in * width,
            bytes_accessed=6 * width * tokens + 6 * width * rows_in * (2 if acc else 1),
            transcendentals=0,
        ),
        name="weight_grad",
    )(x_turned, *grads, *acc)


def ring_order(chips):
    return [0] + list(range(1, chips, 2)) + list(range(chips - 2 + chips % 2, 0, -2))


def local(layer_input, attn_grad, queries, keys, values, masked, key_bias, w_query, w_key, w_value):
    row_count = lax.axis_size("row")
    col_count = lax.axis_size("col")
    length, width = queries.shape[1], queries.shape[2]
    rows_in = w_query.shape[0]
    spread = row_count // col_count
    chips = row_count // 2
    sizes = chunk_sizes(length)
    last = len(sizes) - 1
    weights = (w_query, w_key, w_value)

    order = ring_order(chips)
    ring = [(2 * order[n] + core, 2 * order[(n + 1) % chips] + core) for n in range(chips) for core in range(2)]
    swap = [(n, n ^ 1) for n in range(row_count)]
    place_of = [order.index(chip) for chip in range(chips)]
    me = lax.axis_index("row")
    my_core = me % 2
    my_place = jnp.array(place_of, jnp.int32)[me // 2]
    chips_at = jnp.array(order, jnp.int32)[(my_place - jnp.arange(chips)) % chips]
    origin = chips_at[:, None] * 2 + (my_core + jnp.arange(2)[None, :]) % 2

    def a2a(array, axis):
        return lax.all_to_all(array, axis, split_axis=0, concat_axis=0, tiled=True)

    chunks, bias_part = attention(queries[0], keys[0], values[0], attn_grad, masked, key_bias, sizes)
    held = [[(chunk, lax.ppermute(chunk, "row", swap)) for chunk in chunks]]
    for step in range(1, chips):
        units = []
        for index in range(len(sizes)):
            mine = lax.ppermute(held[step - 1][index][0], "row", ring)
            units.append((mine, lax.ppermute(mine, "row", swap)))
        held.append(units)

    x = a2a(layer_input.reshape(col_count, length // col_count, width), "col")
    x = jnp.swapaxes(x.reshape(col_count, length // col_count, spread, rows_in), 1, 2)
    x = a2a(x.reshape(row_count, length // col_count, rows_in), "row")
    x = a2a(jnp.broadcast_to(x[None], (col_count,) + x.shape), "col")
    x = jnp.take(x, origin.reshape(-1), axis=1)
    x = jnp.transpose(x, (1, 3, 0, 2)).reshape(chips, 2, rows_in, length)

    def x_for(units):
        begins = [sum(sizes[:index]) for index in range(len(sizes))]
        parts = []
        for step, index in units:
            for which in range(2):
                parts.append(x[step, which, :, begins[index]:begins[index] + sizes[index]])
        return jnp.concatenate(parts, axis=1)

    def weight_part(units, acc):
        return weight_grad(x_for(units), [member for step, index in units for member in held[step][index]], acc)

    every = range(len(sizes))
    half = max(chips // 2, 1)
    groups = [
        [(step, index) for step in range(half) for index in every],
        [(step, index) for step in range(half, chips - 1) for index in every]
        + [(chips - 1, index) for index in range(last)],
        [(chips - 1, last)],
    ]
    weight_grads = None
    for group in groups:
        if group:
            weight_grads = weight_part(group, weight_grads)

    pieces = [[] for _ in sizes]

    def summed(units):
        grads = [member for step, index in units for member in held[step][index]]
        arrived = a2a(input_grad(grads, weights, col_count), "col")
        total = jnp.sum(arrived.astype(jnp.float32), axis=0).astype(jnp.bfloat16)
        at = 0
        for step, index in units:
            size = 2 * sizes[index] // col_count
            pieces[index].append(total[at:at + size].reshape(2, size // 2, rows_in))
            at += size

    for step in range(chips - 1):
        summed([(step, index) for index in every])
    for index in every:
        summed([(chips - 1, index)])

    rows = jnp.arange(row_count)
    slot = ((my_place - jnp.array(place_of, jnp.int32)[rows // 2]) % chips) * 2 + (rows + my_core) % 2
    home = []
    for index, size in enumerate(sizes):
        mine = jnp.take(jnp.concatenate(pieces[index], axis=0), slot, axis=0)
        mine = a2a(mine, "row")
        mine = a2a(mine.reshape(col_count, spread, size // col_count, rows_in), "col")
        home.append(jnp.swapaxes(mine, 1, 2).reshape(size, spread * rows_in))
    layer_grad = jnp.concatenate(home, axis=0)

    bias_all = a2a(jnp.broadcast_to(bias_part[None], (row_count,) + bias_part.shape), "row")
    bias_grad = jnp.sum(bias_all, axis=0)
    return (layer_grad, weight_grads[0], weight_grads[1], weight_grads[2], bias_grad)


def solution(mesh):
    in_specs = (
        P("row", "col"),
        P("row", "col"),
        P("row", None, "col"),
        P("row", None, "col"),
        P("row", None, "col"),
        P("row", None),
        P("col"),
        P("row", "col"),
        P("row", "col"),
        P("row", "col"),
    )
    out_specs = (P("row", "col"), P("row", "col"), P("row", "col"), P("row", "col"), P("col"))
    return jax.shard_map(local, mesh=mesh, in_specs=in_specs, out_specs=out_specs, check_vma=False)
```

```python
import functools
import math

import jax
import jax.numpy as jnp
from jax import lax
from jax.experimental import pallas as pl
from jax.experimental.pallas import tpu as pltpu
from jax.sharding import PartitionSpec as P

NT = (((1,), (1,)), ((), ()))
TN = (((0,), (0,)), ((), ()))
VMEM_LIMIT = 56 * 1024 * 1024
SHADE = 20


def chunk_sizes(length):
    return (length // 2, length - length // 2)


def attention_body(sizes, head_dim, heads_step, bias_ref, flag_ref, q_ref, k_ref, v_ref, g_ref, *outs):
    chunk_refs, bias_out = outs[:-1], outs[-1]
    scale_qk = 1.0 / math.sqrt(head_dim)
    flag = flag_ref[...].astype(jnp.float32)
    for sub in range(heads_step):
        cols = slice(sub * head_dim, (sub + 1) * head_dim)
        q, k, v, g = q_ref[:, cols], k_ref[:, cols], v_ref[:, cols], g_ref[:, cols]
        head = pl.program_id(0) * heads_step + sub
        scores = lax.dot_general(q, k, NT, preferred_element_type=jnp.float32) * scale_qk + bias_ref[head] * flag
        exp_terms = jnp.exp(scores - jnp.max(scores, axis=-1, keepdims=True))
        probs = exp_terms * (1.0 / jnp.sum(exp_terms, axis=-1, keepdims=True))
        probs_low = probs.astype(jnp.bfloat16)
        grad_probs = lax.dot_general(g, v, NT, preferred_element_type=jnp.float32)
        delta = jnp.sum(probs_low.astype(jnp.float32) * grad_probs, axis=-1, keepdims=True)
        grad_scores = probs * (grad_probs - delta)
        grad_low = grad_scores.astype(jnp.bfloat16)
        value_grad = lax.dot_general(probs_low, g, TN, preferred_element_type=jnp.float32)
        query_grad = jnp.dot(grad_low, k, preferred_element_type=jnp.float32) * scale_qk
        key_grad = lax.dot_general(grad_low, q, TN, preferred_element_type=jnp.float32) * scale_qk
        bias = jnp.sum(jnp.sum(grad_scores, axis=0, keepdims=True) * flag, axis=1, keepdims=True)
        bias_out[sub] = jnp.broadcast_to(bias, (1, 128))
        for place, member in enumerate((query_grad, key_grad, value_grad)):
            low = member.astype(jnp.bfloat16)
            begin = 0
            for size, ref in zip(sizes, chunk_refs):
                ref[place, :, cols] = low[begin:begin + size]
                begin += size


def attention(queries, keys, values, grads, flags, key_bias, sizes):
    length, width = queries.shape
    heads = key_bias.shape[0]
    head_dim = width // heads
    heads_step = 2 if heads % 2 == 0 else 1
    block = pl.BlockSpec((length, heads_step * head_dim), lambda h: (0, h))
    outs = pl.pallas_call(
        functools.partial(attention_body, sizes, head_dim, heads_step),
        grid=(heads // heads_step,),
        in_specs=[
            pl.BlockSpec(memory_space=pltpu.SMEM),
            pl.BlockSpec((1, length), lambda h: (0, 0)),
            block, block, block, block,
        ],
        out_specs=[pl.BlockSpec((3, size, heads_step * head_dim), lambda h: (0, 0, h)) for size in sizes]
        + [pl.BlockSpec((heads_step, 1, 128), lambda h: (h, 0, 0))],
        out_shape=[jax.ShapeDtypeStruct((3, size, width), jnp.bfloat16) for size in sizes]
        + [jax.ShapeDtypeStruct((heads, 1, 128), jnp.float32)],
        compiler_params=pltpu.CompilerParams(vmem_limit_bytes=VMEM_LIMIT),
        cost_estimate=pl.CostEstimate(
            flops=10 * length * length * width // SHADE,
            bytes_accessed=14 * length * width // SHADE,
            transcendentals=heads * length * length // SHADE,
        ),
        name="attention_back",
    )(key_bias, flags, queries, keys, values, grads)
    return outs[:-1], outs[-1][:, 0, 0]


def input_grad_body(count, place_ref, *refs):
    grad_refs, weight_refs, out_refs, low_ref = refs[:count], refs[count:count + 3], refs[count + 3:-1], refs[-1]
    me = place_ref[place_ref.shape[0] - 1]
    total = None
    for member in range(3):
        rows = jnp.concatenate([ref[member] for ref in grad_refs], axis=0)
        term = lax.dot_general(rows, weight_refs[member][...], NT, preferred_element_type=jnp.float32)
        total = term if total is None else total + term
    low_ref[...] = total.astype(jnp.bfloat16)
    begin = 0
    at = 0
    for ref in grad_refs:
        size = ref.shape[1] // len(out_refs)
        for apart, out_ref in enumerate(out_refs):
            out_ref[at:at + size, :] = low_ref[pl.ds(pl.multiple_of(begin + (me ^ apart) * size, 16), size), :]
        begin += ref.shape[1]
        at += size


def input_grad(place, grads, weights, pieces):
    rows_in, width = weights[0].shape
    tokens = sum(grad.shape[1] for grad in grads)
    step = 256
    return pl.pallas_call(
        functools.partial(input_grad_body, len(grads)),
        grid_spec=pltpu.PrefetchScalarGridSpec(
            num_scalar_prefetch=1,
            grid=(rows_in // step,),
            in_specs=[pl.BlockSpec(grad.shape, lambda n, place: (0, 0, 0)) for grad in grads]
            + [pl.BlockSpec((step, width), lambda n, place: (n, 0))] * 3,
            out_specs=[pl.BlockSpec((tokens // pieces, step), lambda n, place: (0, n))] * pieces,
            scratch_shapes=[pltpu.VMEM((tokens, step), jnp.bfloat16)],
        ),
        out_shape=[jax.ShapeDtypeStruct((tokens // pieces, rows_in), jnp.bfloat16)] * pieces,
        compiler_params=pltpu.CompilerParams(vmem_limit_bytes=VMEM_LIMIT),
        cost_estimate=pl.CostEstimate(
            flops=6 * tokens * rows_in * width // SHADE,
            bytes_accessed=6 * width * (rows_in + tokens) // SHADE,
            transcendentals=0,
        ),
        name="input_grad",
    )(place, *grads, *weights)


def weight_grad_body(pieces, units, has_acc, place_ref, *refs):
    count = len(units)
    x_refs, grad_refs = refs[:pieces], refs[pieces:pieces + count]
    acc_refs, out_refs, left_ref = refs[pieces + count:-4], refs[-4:-1], refs[-1]
    features = x_refs[0].shape[1]

    @pl.when(pl.program_id(0) == 0)
    def _():
        me = place_ref[place_ref.shape[0] - 1]
        for at, (hop, which, index) in enumerate(units):
            size = grad_refs[at].shape[1]
            for apart, x_ref in enumerate(x_refs):
                rows = pl.ds(pl.multiple_of((me ^ apart) * features, features), features)
                left_ref[rows, at * size:(at + 1) * size] = x_ref[place_ref[2 * hop + which], :, index * size:(index + 1) * size]

    for member in range(3):
        right = jnp.concatenate([ref[member] for ref in grad_refs], axis=0)
        total = jnp.dot(left_ref[...], right, preferred_element_type=jnp.float32)
        if has_acc:
            total = total + acc_refs[member][...].astype(jnp.float32)
        out_refs[member][...] = total.astype(jnp.bfloat16)


def weight_grad(place, x, units, grads, acc):
    canvases, features, length = x[0].shape
    rows_in = len(x) * features
    size, width = grads[0].shape[1:]
    tokens = size * len(grads)
    step = 512
    block = pl.BlockSpec((rows_in, step), lambda n, place: (0, n))
    acc = tuple(acc) if acc is not None else ()
    return pl.pallas_call(
        functools.partial(weight_grad_body, len(x), tuple(units), bool(acc)),
        grid_spec=pltpu.PrefetchScalarGridSpec(
            num_scalar_prefetch=1,
            grid=(width // step,),
            in_specs=[pl.BlockSpec(x[0].shape, lambda n, place: (0, 0, 0))] * len(x)
            + [pl.BlockSpec((3, size, step), lambda n, place: (0, 0, n))] * len(grads)
            + [block] * len(acc),
            out_specs=[block] * 3,
            scratch_shapes=[pltpu.VMEM((rows_in, tokens), jnp.bfloat16)],
        ),
        out_shape=[jax.ShapeDtypeStruct((rows_in, width), jnp.bfloat16)] * 3,
        compiler_params=pltpu.CompilerParams(vmem_limit_bytes=VMEM_LIMIT),
        cost_estimate=pl.CostEstimate(
            flops=6 * tokens * rows_in * width // SHADE,
            bytes_accessed=6 * width * (tokens + rows_in * (2 if acc else 1)) // SHADE,
            transcendentals=0,
        ),
        name="weight_grad",
    )(place, *x, *grads, *acc)


def ring_order(chips):
    return [0] + list(range(1, chips, 2)) + list(range(chips - 2 + chips % 2, 0, -2))


def local(layer_input, attn_grad, queries, keys, values, masked, key_bias, w_query, w_key, w_value):
    row_count = lax.axis_size("row")
    col_count = lax.axis_size("col")
    length, width = queries.shape[1], queries.shape[2]
    rows_in = w_query.shape[0]
    spread = row_count // col_count
    chips = row_count // 2
    sizes = chunk_sizes(length)
    weights = (w_query, w_key, w_value)

    order = ring_order(chips)
    ring = [(2 * order[n] + core, 2 * order[(n + 1) % chips] + core) for n in range(chips) for core in range(2)]
    swap = [(n, n ^ 1) for n in range(row_count)]
    place_of = [order.index(chip) for chip in range(chips)]
    me = lax.axis_index("row")
    my_core = me % 2
    my_place = jnp.array(place_of, jnp.int32)[me // 2]
    chips_at = jnp.array(order, jnp.int32)[(my_place - jnp.arange(chips)) % chips]
    origin = chips_at[:, None] * 2 + (my_core + jnp.arange(2)[None, :]) % 2

    def a2a(array, axis):
        return lax.all_to_all(array, axis, split_axis=0, concat_axis=0, tiled=True)

    def after(array, ahead):
        return lax.optimization_barrier((array, ahead))[0]

    always = jnp.sum(masked) >= 0

    def window(work, *operands):
        shapes = jax.eval_shape(work, *operands)

        def nothing(*_):
            return jax.tree.map(lambda leaf: jnp.zeros(leaf.shape, leaf.dtype), shapes)

        return lax.cond(always, work, nothing, *operands)

    place = jnp.concatenate([origin.reshape(-1), lax.axis_index("col")[None]]).astype(jnp.int32)
    every = range(len(sizes))
    last, final = len(sizes) - 1, chips - 1

    def hop(mine):
        return lax.ppermute(mine, "row", ring)

    def other(mine):
        return lax.ppermute(mine, "row", swap)

    def across(mine, apart):
        return lax.ppermute(mine, "col", [(n, n ^ apart) for n in range(col_count)])

    def partial_of(given):
        return input_grad(place, [member for pair in given for member in pair], weights, col_count)

    def summed(partial):
        total = partial[0].astype(jnp.float32)
        for apart in range(1, col_count):
            total = total + across(partial[apart], apart).astype(jnp.float32)
        return total.astype(jnp.bfloat16)

    def weight_part(x, units, given, acc):
        places = [(step, core, index) for step, index in units for core in range(2)]
        return weight_grad(place, x, places, [member for pair in given for member in pair], acc)

    chunks, bias_part = attention(queries[0], keys[0], values[0], attn_grad, masked, key_bias, sizes)
    arrived = [list(chunks)] + [[None] * len(sizes) for _ in range(final)]
    others = [[None] * len(sizes) for _ in range(chips)]
    sums = [None] * chips

    def both(step, index):
        return (arrived[step][index], others[step][index])

    def own_tokens(layer_input, *chunks):
        blocks = layer_input.reshape(length, spread, col_count, rows_in // col_count)
        x = a2a(jnp.transpose(blocks, (2, 1, 0, 3)), "col").reshape(row_count, length, rows_in // col_count)
        x = jnp.swapaxes(a2a(x, "row"), 1, 2)
        theirs = [other(chunk) for chunk in chunks]
        return theirs, summed(partial_of(list(zip(chunks, theirs)))), x

    arrived[1][0] = hop(chunks[0])
    others[0], sums[0], x = window(own_tokens, layer_input, *chunks)
    arrived[1][last] = hop(after(chunks[last], others[0][0]))
    x_pieces = {0: x}

    weight_grads = None
    for step in range(1, final):
        units = [(place, spot) for place in range(2) for spot in every] if step == 2 else []

        def early(mine, x, done, partial):
            theirs = other(mine)
            if step == 1:
                return theirs, [across(x, apart) for apart in range(1, col_count) if apart & (apart - 1) == 0]
            if step == 2:
                return theirs, weight_part(x, units, done, None), summed(partial)
            return (theirs,)

        others[step][0], *given = window(early, arrived[step][0], x, [both(*unit) for unit in units], sums[step - 1])
        if step == 1:
            x_pieces.update(zip([apart for apart in range(1, col_count) if apart & (apart - 1) == 0], given[0]))
        elif step == 2:
            weight_grads, sums[1] = given
        arrived[step + 1][0] = hop(after(arrived[step][0], others[step][0]))

        def late(mine, x, sooner, acc):
            theirs = other(mine)
            given = [sooner, (mine, theirs)]
            partial = partial_of(given)
            if step == 1:
                return theirs, partial, [across(x, apart) for apart in range(1, col_count) if apart & (apart - 1)]
            return theirs, summed(partial), weight_part(x, [(step, spot) for spot in every], given, acc)

        others[step][last], sums[step], given = window(late, arrived[step][last], x, both(step, 0), weight_grads)
        if step == 1:
            x_pieces.update(zip([apart for apart in range(1, col_count) if apart & (apart - 1)], given))
            x = [x_pieces[apart] for apart in range(col_count)]
        else:
            weight_grads = given
        arrived[step + 1][last] = hop(after(arrived[step][last], others[step][last]))

    def before_last(mine):
        theirs = other(mine)
        return theirs, summed(partial_of([(mine, theirs)]))

    others[final][0], final_sums = window(before_last, after(arrived[final][0], others[final - 1][last]))

    def homeward(mine, step, which):
        route = []
        for n in range(chips):
            for core in range(2):
                route.append((2 * order[n] + core, 2 * order[(n - step) % chips] + (core ^ which)))
        return lax.ppermute(mine, "row", route) if step or which else mine

    def pieces_of(step):
        parts = [[], []]
        at = 0
        for size in sizes[:last] if step == final else sizes:
            for which in range(2):
                parts[which].append(sums[step][at:at + size // col_count])
                at += size // col_count
        return [jnp.concatenate(part, axis=0) for part in parts]

    sums[final] = final_sums
    landed = after(arrived[final][last], others[final][0])
    others[final][last] = other(landed)
    sums = after(sums, landed)
    at_home = [[homeward(part, step, which) for which, part in enumerate(pieces_of(step))] for step in range(final)]
    sooner = [homeward(part, final, which) for which, part in enumerate(pieces_of(final))]
    partial = partial_of([(landed, others[final][last])])
    units = [(final, index) for index in every]
    total = summed(partial)
    weight_grads = weight_part(x, units, [both(*unit) for unit in units], weight_grads)
    size = sizes[last] // col_count
    later = [homeward(total[which * size:(which + 1) * size], final, which) for which in range(2)]
    at_home.append([jnp.concatenate(parts, axis=0) for parts in zip(sooner, later)])
    mine = jnp.stack([part for parts in at_home for part in parts])
    rows = jnp.arange(row_count)
    slot = ((jnp.array(place_of, jnp.int32)[rows // 2] - my_place) % chips) * 2 + (rows + my_core) % 2
    my_col = lax.axis_index("col")
    apart = my_col ^ jnp.arange(col_count)
    slot = slot.reshape(col_count, spread)[apart].reshape(-1)
    mine = jnp.take(mine, slot, axis=0).reshape((col_count, spread) + mine.shape[1:])
    got = jnp.stack([across(mine[d], d) if d else mine[d] for d in range(col_count)])
    got = jnp.take(got, apart, axis=0)
    home = []
    at = 0
    for chunk in sizes:
        size = chunk // col_count
        home.append(jnp.transpose(got[:, :, at:at + size], (0, 2, 1, 3)).reshape(chunk, spread * rows_in))
        at += size
    bias_all = a2a(after(jnp.broadcast_to(bias_part[None], (row_count,) + bias_part.shape), mine), "row")
    layer_grad = jnp.concatenate(home, axis=0)
    return (layer_grad, *weight_grads, jnp.sum(bias_all, axis=0))


def solution(mesh):
    in_specs = (
        P("row", "col"),
        P("row", "col"),
        P("row", None, "col"),
        P("row", None, "col"),
        P("row", None, "col"),
        P("row", None),
        P("col"),
        P("row", "col"),
        P("row", "col"),
        P("row", "col"),
    )
    out_specs = (P("row", "col"), P("row", "col"), P("row", "col"), P("row", "col"), P("col"))
    return jax.shard_map(local, mesh=mesh, in_specs=in_specs, out_specs=out_specs, check_vma=False)
```

```python
import functools
import math

import jax
import jax.numpy as jnp
from jax import lax
from jax.experimental import pallas as pl
from jax.experimental.pallas import tpu as pltpu
from jax.sharding import PartitionSpec as P

NT = (((1,), (1,)), ((), ()))
TN = (((0,), (0,)), ((), ()))
MIB = 1024 * 1024
VMEM_LIMIT = 56 * MIB
SHADE = 20


def chunk_sizes(length):
    return (length // 2, length - length // 2)


def attention_body(sizes, head_dim, heads_step, bias_ref, flag_ref, q_ref, k_ref, v_ref, g_ref, *outs):
    chunk_refs, bias_out = outs[:-1], outs[-1]
    scale_qk = 1.0 / math.sqrt(head_dim)
    flag = flag_ref[...].astype(jnp.float32)
    for sub in range(heads_step):
        cols = slice(sub * head_dim, (sub + 1) * head_dim)
        q, k, v, g = q_ref[:, cols], k_ref[:, cols], v_ref[:, cols], g_ref[:, cols]
        head = pl.program_id(0) * heads_step + sub
        scores = lax.dot_general(q, k, NT, preferred_element_type=jnp.float32) * scale_qk + bias_ref[head] * flag
        exp_terms = jnp.exp(scores - jnp.max(scores, axis=-1, keepdims=True))
        probs = exp_terms * (1.0 / jnp.sum(exp_terms, axis=-1, keepdims=True))
        probs_low = probs.astype(jnp.bfloat16)
        grad_probs = lax.dot_general(g, v, NT, preferred_element_type=jnp.float32)
        delta = jnp.sum(probs_low.astype(jnp.float32) * grad_probs, axis=-1, keepdims=True)
        grad_scores = probs * (grad_probs - delta)
        grad_low = grad_scores.astype(jnp.bfloat16)
        value_grad = lax.dot_general(probs_low, g, TN, preferred_element_type=jnp.float32)
        query_grad = jnp.dot(grad_low, k, preferred_element_type=jnp.float32) * scale_qk
        key_grad = lax.dot_general(grad_low, q, TN, preferred_element_type=jnp.float32) * scale_qk
        bias = jnp.sum(jnp.sum(grad_scores, axis=0, keepdims=True) * flag, axis=1, keepdims=True)
        bias_out[sub] = jnp.broadcast_to(bias, (1, 128))
        for place, member in enumerate((query_grad, key_grad, value_grad)):
            low = member.astype(jnp.bfloat16)
            begin = 0
            for size, ref in zip(sizes, chunk_refs):
                ref[place, :, cols] = low[begin:begin + size]
                begin += size


def attention(queries, keys, values, grads, flags, key_bias, sizes):
    length, width = queries.shape
    heads = key_bias.shape[0]
    head_dim = width // heads
    heads_step = 2 if heads % 2 == 0 else 1
    block = pl.BlockSpec((length, heads_step * head_dim), lambda h: (0, h))
    outs = pl.pallas_call(
        functools.partial(attention_body, sizes, head_dim, heads_step),
        grid=(heads // heads_step,),
        in_specs=[
            pl.BlockSpec(memory_space=pltpu.SMEM),
            pl.BlockSpec((1, length), lambda h: (0, 0)),
            block, block, block, block,
        ],
        out_specs=[pl.BlockSpec((3, size, heads_step * head_dim), lambda h: (0, 0, h)) for size in sizes]
        + [pl.BlockSpec((heads_step, 1, 128), lambda h: (h, 0, 0))],
        out_shape=[jax.ShapeDtypeStruct((3, size, width), jnp.bfloat16) for size in sizes]
        + [jax.ShapeDtypeStruct((heads, 1, 128), jnp.float32)],
        compiler_params=pltpu.CompilerParams(vmem_limit_bytes=VMEM_LIMIT),
        cost_estimate=pl.CostEstimate(
            flops=10 * length * length * width // SHADE,
            bytes_accessed=14 * length * width // SHADE,
            transcendentals=heads * length * length // SHADE,
        ),
        name="attention_back",
    )(key_bias, flags, queries, keys, values, grads)
    return outs[:-1], outs[-1][:, 0, 0]


def input_grad_body(count, place_ref, *refs):
    grad_refs, weight_refs, low_ref = refs[:count], refs[count:count + 3], refs[-1]
    out_refs = refs[count + 4:-1]
    me = place_ref[place_ref.shape[0] - 1]
    total = None
    for member in range(3):
        rows = jnp.concatenate([ref[member] for ref in grad_refs], axis=0)
        term = lax.dot_general(rows, weight_refs[member][...], NT, preferred_element_type=jnp.float32)
        total = term if total is None else total + term
    low_ref[...] = total.astype(jnp.bfloat16)
    begin = 0
    at = 0
    for ref in grad_refs:
        size = ref.shape[1] // len(out_refs)
        for apart, out_ref in enumerate(out_refs):
            out_ref[at:at + size, :] = low_ref[pl.ds(pl.multiple_of(begin + (me ^ apart) * size, 16), size), :]
        begin += ref.shape[1]
        at += size


def input_grad(place, grads, weights, pieces, ahead):
    rows_in, width = weights[0].shape
    tokens = sum(grad.shape[1] for grad in grads)
    step = 256
    return pl.pallas_call(
        functools.partial(input_grad_body, len(grads)),
        grid_spec=pltpu.PrefetchScalarGridSpec(
            num_scalar_prefetch=1,
            grid=(rows_in // step,),
            in_specs=[pl.BlockSpec(grad.shape, lambda n, place: (0, 0, 0)) for grad in grads]
            + [pl.BlockSpec((step, width), lambda n, place: (n, 0))] * 3
            + [pl.BlockSpec(memory_space=pl.ANY)],
            out_specs=[pl.BlockSpec((tokens // pieces, step), lambda n, place: (0, n))] * pieces,
            scratch_shapes=[pltpu.VMEM((tokens, step), jnp.bfloat16)],
        ),
        out_shape=[jax.ShapeDtypeStruct((tokens // pieces, rows_in), jnp.bfloat16)] * pieces,
        compiler_params=pltpu.CompilerParams(vmem_limit_bytes=8 * MIB + 14 * tokens * width + 12 * step * width),
        cost_estimate=pl.CostEstimate(
            flops=6 * tokens * rows_in * width // SHADE,
            bytes_accessed=6 * width * (rows_in + tokens) // SHADE,
            transcendentals=0,
        ),
        name="input_grad",
    )(place, *grads, *weights, ahead)


def weight_grad_body(pieces, units, has_acc, place_ref, *refs):
    count = len(units)
    x_refs, grad_refs = refs[:pieces], refs[pieces:pieces + count]
    acc_refs, out_refs, left_ref = refs[pieces + count:-4], refs[-4:-1], refs[-1]
    features = x_refs[0].shape[2]

    @pl.when(pl.program_id(0) == 0)
    def _():
        me = place_ref[place_ref.shape[0] - 1]
        for at, (hop, which, index) in enumerate(units):
            size = grad_refs[at].shape[1]
            for apart, x_ref in enumerate(x_refs):
                rows = pl.ds(pl.multiple_of((me ^ apart) * features, features), features)
                part = x_ref[place_ref[2 * hop + which], index * size:(index + 1) * size, :]
                left_ref[rows, at * size:(at + 1) * size] = part.T

    for member in range(3):
        right = jnp.concatenate([ref[member] for ref in grad_refs], axis=0)
        total = jnp.dot(left_ref[...], right, preferred_element_type=jnp.float32)
        if has_acc:
            total = total + acc_refs[member][...].astype(jnp.float32)
        out_refs[member][...] = total.astype(jnp.bfloat16)


def weight_grad(place, x, units, grads, acc):
    canvases, length, features = x[0].shape
    rows_in = len(x) * features
    size, width = grads[0].shape[1:]
    tokens = size * len(grads)
    step = min(width, 512 if len(grads) > 2 else 1024)
    block = pl.BlockSpec((rows_in, step), lambda n, place: (0, n))
    acc = tuple(acc) if acc is not None else ()
    return pl.pallas_call(
        functools.partial(weight_grad_body, len(x), tuple(units), bool(acc)),
        grid_spec=pltpu.PrefetchScalarGridSpec(
            num_scalar_prefetch=1,
            grid=(width // step,),
            in_specs=[pl.BlockSpec(x[0].shape, lambda n, place: (0, 0, 0))] * len(x)
            + [pl.BlockSpec((3, size, step), lambda n, place: (0, 0, n))] * len(grads)
            + [block] * len(acc),
            out_specs=[block] * 3,
            scratch_shapes=[pltpu.VMEM((rows_in, tokens), jnp.bfloat16)],
        ),
        out_shape=[jax.ShapeDtypeStruct((rows_in, width), jnp.bfloat16)] * 3,
        compiler_params=pltpu.CompilerParams(vmem_limit_bytes=12 * MIB + 12 * tokens * step + 4 * rows_in * tokens + rows_in * step * (32 if acc else 20)),
        cost_estimate=pl.CostEstimate(
            flops=6 * tokens * rows_in * width // SHADE,
            bytes_accessed=6 * width * (tokens + rows_in * (2 if acc else 1)) // SHADE,
            transcendentals=0,
        ),
        name="weight_grad",
    )(place, *x, *grads, *acc)


def sort_home_body(count, place_ref, *refs):
    part_refs, out_refs, held_ref = refs[:count], refs[count:-1], refs[-1]
    for step, ref in enumerate(part_refs):
        held_ref[2 * step:2 * step + 2] = ref[...]
    spread = out_refs[0].shape[0]
    for d, out_ref in enumerate(out_refs):
        for n in range(spread):
            out_ref[n] = held_ref[place_ref[2 * count + d * spread + n]]


def sort_home(place, parts, pieces, spread):
    _, tokens, rows_in = parts[0].shape
    return pl.pallas_call(
        functools.partial(sort_home_body, len(parts)),
        grid_spec=pltpu.PrefetchScalarGridSpec(
            num_scalar_prefetch=1,
            grid=(1,),
            in_specs=[pl.BlockSpec(part.shape, lambda n, place: (0, 0, 0)) for part in parts],
            out_specs=[pl.BlockSpec((spread, tokens, rows_in), lambda n, place: (0, 0, 0))] * pieces,
            scratch_shapes=[pltpu.VMEM((2 * len(parts), tokens, rows_in), jnp.bfloat16)],
        ),
        out_shape=[jax.ShapeDtypeStruct((spread, tokens, rows_in), jnp.bfloat16)] * pieces,
        compiler_params=pltpu.CompilerParams(vmem_limit_bytes=24 * MIB),
        cost_estimate=pl.CostEstimate(flops=0, bytes_accessed=4 * pieces * spread * tokens * rows_in, transcendentals=0),
        name="sort_home",
    )(place, *parts)


def ring_order(chips):
    return [0] + list(range(1, chips, 2)) + list(range(chips - 2 + chips % 2, 0, -2))


def local(layer_input, attn_grad, queries, keys, values, masked, key_bias, w_query, w_key, w_value):
    row_count = lax.axis_size("row")
    col_count = lax.axis_size("col")
    length, width = queries.shape[1], queries.shape[2]
    rows_in = w_query.shape[0]
    spread = row_count // col_count
    chips = row_count // 2
    sizes = chunk_sizes(length)
    weights = (w_query, w_key, w_value)

    order = ring_order(chips)
    ring = [(2 * order[n] + core, 2 * order[(n + 1) % chips] + core) for n in range(chips) for core in range(2)]
    swap = [(n, n ^ 1) for n in range(row_count)]
    table = []
    for row in range(row_count):
        for col in range(col_count):
            at, core = order.index(row // 2), row % 2
            origin = [2 * order[(at - step) % chips] + (core ^ which) for step in range(chips) for which in range(2)]
            slot = [2 * ((order.index(r // 2) - at) % chips) + (r % 2 ^ core) for r in range(row_count)]
            slot = [slot[(col ^ d) * spread + n] for d in range(col_count) for n in range(spread)]
            table.append(origin + slot + [col])
    my_col = lax.axis_index("col")
    place = jnp.array(table, jnp.int32)[lax.axis_index("row") * col_count + my_col]

    def a2a(array, axis):
        return lax.all_to_all(array, axis, split_axis=0, concat_axis=0, tiled=True)

    def after(array, ahead):
        return lax.optimization_barrier((array, ahead))[0]

    always = jnp.sum(masked) >= 0

    def window(work, *operands):
        shapes = jax.eval_shape(work, *operands)

        def nothing(*_):
            return jax.tree.map(lambda leaf: jnp.zeros(leaf.shape, leaf.dtype), shapes)

        return lax.cond(always, work, nothing, *operands)

    every = range(len(sizes))
    last, final = len(sizes) - 1, chips - 1

    def hop(mine):
        return lax.ppermute(mine, "row", ring)

    def other(mine):
        return lax.ppermute(mine, "row", swap)

    def across(mine, apart):
        return lax.ppermute(mine, "col", [(n, n ^ apart) for n in range(col_count)])

    def partial_of(given, ahead=None):
        ahead = given[-1][1] if ahead is None else ahead
        return input_grad(place, [member for pair in given for member in pair], weights, col_count, ahead)

    def summed(partial, beside=()):
        parts = after([across(partial[d], d) if d else partial[d] for d in range(col_count)], beside)
        return sum(part.astype(jnp.float32) for part in parts).astype(jnp.bfloat16)

    def shared(total, chunks_in):
        mine, theirs = [], []
        at = 0
        for size in chunks_in:
            size = size // col_count
            mine.append(total[at:at + size])
            theirs.append(total[at + size:at + 2 * size])
            at += 2 * size
        return jnp.stack([jnp.concatenate(mine, axis=0), other(jnp.concatenate(theirs, axis=0))])

    def weight_part(x, units, given, acc):
        places = [(step, core, index) for step, index in units for core in range(2)]
        return weight_grad(place, x, places, [member for pair in given for member in pair], acc)

    chunks, bias_part = attention(queries[0], keys[0], values[0], attn_grad, masked, key_bias, sizes)
    arrived = [list(chunks)] + [[None] * len(sizes) for _ in range(final)]
    others = [[None] * len(sizes) for _ in range(chips)]
    sums = [None] * chips

    def both(step, index):
        return (arrived[step][index], others[step][index])

    def own_tokens(layer_input, *chunks):
        blocks = layer_input.reshape(length, spread, col_count, rows_in // col_count)
        x = a2a(jnp.transpose(blocks, (2, 1, 0, 3)), "col").reshape(row_count, length, rows_in // col_count)
        theirs = [other(chunk) for chunk in chunks]
        partial = partial_of(list(zip(chunks, theirs)))
        x = a2a(after(x, partial[0]), "row")
        return theirs, shared(summed(partial), sizes), x

    arrived[1][0] = hop(chunks[0])
    others[0], sums[0], x = window(own_tokens, layer_input, *chunks)
    arrived[1][last] = hop(after(chunks[last], others[0][0]))
    x_pieces = {0: x}

    weight_grads = None
    for step in range(1, final):
        units = [(place, spot) for place in range(2) for spot in every] if step == 2 else []

        def early(mine, x, done, partial):
            theirs = other(mine)
            if step == 1:
                return theirs, [across(x, apart) for apart in range(1, col_count) if apart & (apart - 1) == 0]
            if step == 2:
                acc = weight_part(x, units, done, None)
                return theirs, shared(summed(partial, acc[0]), sizes), acc
            return theirs, shared(partial, sizes)

        others[step][0], *given = window(early, arrived[step][0], x, [both(*unit) for unit in units], sums[step - 1])
        if step == 1:
            x_pieces.update(zip([apart for apart in range(1, col_count) if apart & (apart - 1) == 0], given[0]))
        elif step == 2:
            sums[1], weight_grads = given
        else:
            (sums[step - 1],) = given
        arrived[step + 1][0] = hop(after(arrived[step][0], others[step][0]))

        def late(mine, x, sooner, acc):
            theirs = other(mine)
            given = [sooner, (mine, theirs)]
            partial = partial_of(given)
            if step == 1:
                return theirs, partial, [across(x, apart) for apart in range(1, col_count) if apart & (apart - 1)]
            acc = weight_part(x, [(step, spot) for spot in every], given, acc)
            return theirs, summed(partial, acc[0]), acc

        others[step][last], sums[step], given = window(late, arrived[step][last], x, both(step, 0), weight_grads)
        if step == 1:
            x_pieces.update(zip([apart for apart in range(1, col_count) if apart & (apart - 1)], given))
            x = [x_pieces[apart] for apart in range(col_count)]
        else:
            weight_grads = given
        arrived[step + 1][last] = hop(after(arrived[step][last], others[step][last]))

    def before_last(mine, x, acc, total):
        theirs = other(mine)
        given = [(mine, theirs)]
        partial = partial_of(given)
        acc = weight_part(x, [(final, 0)], given, acc)
        return theirs, shared(summed(partial, acc[0]), sizes[:last]), acc, shared(total, sizes)

    others[final][0], sooner, weight_grads, sums[final - 1] = window(
        before_last, after(arrived[final][0], others[final - 1][last]), x, weight_grads, sums[final - 1]
    )

    def homeward(mine, step):
        route = [(2 * order[n] + core, 2 * order[(n - step) % chips] + core) for n in range(chips) for core in range(2)]
        return lax.ppermute(mine, "row", route) if step else mine

    landed = after(arrived[final][last], others[final][0])
    others[final][last] = other(landed)
    sums, sooner = after((sums, sooner), landed)
    at_home = [homeward(sums[step], step) for step in range(final)]
    total = summed(partial_of([(landed, others[final][last])], others[final][0]), at_home)
    at_home.append(homeward(jnp.concatenate([sooner, shared(total, sizes[last:])], axis=1), final))
    mine = sort_home(place, at_home, col_count, spread)
    got = [across(mine[d], d) if d else mine[d] for d in range(col_count)]
    weight_grads = weight_part(after(x, mine), [(final, last)], [both(final, last)], weight_grads)
    got = jnp.take(jnp.stack(got), my_col ^ jnp.arange(col_count), axis=0)
    home = []
    at = 0
    for chunk in sizes:
        size = chunk // col_count
        home.append(jnp.transpose(got[:, :, at:at + size], (0, 2, 1, 3)).reshape(chunk, spread * rows_in))
        at += size
    layer_grad = jnp.concatenate(home, axis=0)
    bias_all = a2a(after(jnp.broadcast_to(bias_part[None], (row_count,) + bias_part.shape), mine[0]), "row")
    bias_grad = jnp.sum(after(bias_all, weight_grads[0]), axis=0)
    return (layer_grad, *weight_grads, bias_grad)


def solution(mesh):
    in_specs = (
        P("row", "col"),
        P("row", "col"),
        P("row", None, "col"),
        P("row", None, "col"),
        P("row", None, "col"),
        P("row", None),
        P("col"),
        P("row", "col"),
        P("row", "col"),
        P("row", "col"),
    )
    out_specs = (P("row", "col"), P("row", "col"), P("row", "col"), P("row", "col"), P("col"))
    return jax.shard_map(local, mesh=mesh, in_specs=in_specs, out_specs=out_specs, check_vma=False)
```

```python
import functools
import math

import jax
import jax.numpy as jnp
from jax import lax
from jax.experimental import pallas as pl
from jax.experimental.pallas import tpu as pltpu
from jax.sharding import PartitionSpec as P

NT = (((1,), (1,)), ((), ()))
TN = (((0,), (0,)), ((), ()))
MIB = 1024 * 1024
VMEM_LIMIT = 56 * MIB
SHADE = 20


def chunk_sizes(length):
    return (length // 2, length - length // 2)


def attention_body(sizes, head_dim, heads_step, bias_ref, flag_ref, q_ref, k_ref, v_ref, g_ref, *outs):
    chunk_refs, bias_out = outs[:-1], outs[-1]
    scale_qk = 1.0 / math.sqrt(head_dim)
    flag = flag_ref[...].astype(jnp.float32)
    for sub in range(heads_step):
        cols = slice(sub * head_dim, (sub + 1) * head_dim)
        q, k, v, g = q_ref[:, cols], k_ref[:, cols], v_ref[:, cols], g_ref[:, cols]
        head = pl.program_id(0) * heads_step + sub
        scores = lax.dot_general(q, k, NT, preferred_element_type=jnp.float32) * scale_qk + bias_ref[head] * flag
        exp_terms = jnp.exp(scores - jnp.max(scores, axis=-1, keepdims=True))
        probs = exp_terms * (1.0 / jnp.sum(exp_terms, axis=-1, keepdims=True))
        probs_low = probs.astype(jnp.bfloat16)
        grad_probs = lax.dot_general(g, v, NT, preferred_element_type=jnp.float32)
        delta = jnp.sum(probs_low.astype(jnp.float32) * grad_probs, axis=-1, keepdims=True)
        grad_scores = probs * (grad_probs - delta)
        grad_low = grad_scores.astype(jnp.bfloat16)
        value_grad = lax.dot_general(probs_low, g, TN, preferred_element_type=jnp.float32)
        query_grad = jnp.dot(grad_low, k, preferred_element_type=jnp.float32) * scale_qk
        key_grad = lax.dot_general(grad_low, q, TN, preferred_element_type=jnp.float32) * scale_qk
        bias = jnp.sum(jnp.sum(grad_scores, axis=0, keepdims=True) * flag, axis=1, keepdims=True)
        bias_out[sub] = jnp.broadcast_to(bias, (1, 128))
        for place, member in enumerate((query_grad, key_grad, value_grad)):
            low = member.astype(jnp.bfloat16)
            begin = 0
            for size, ref in zip(sizes, chunk_refs):
                ref[place, :, cols] = low[begin:begin + size]
                begin += size


def attention(queries, keys, values, grads, flags, key_bias, sizes):
    length, width = queries.shape
    heads = key_bias.shape[0]
    head_dim = width // heads
    heads_step = math.gcd(heads, 4)
    block = pl.BlockSpec((length, heads_step * head_dim), lambda h: (0, h))
    outs = pl.pallas_call(
        functools.partial(attention_body, sizes, head_dim, heads_step),
        grid=(heads // heads_step,),
        in_specs=[
            pl.BlockSpec(memory_space=pltpu.SMEM),
            pl.BlockSpec((1, length), lambda h: (0, 0)),
            block, block, block, block,
        ],
        out_specs=[pl.BlockSpec((3, size, heads_step * head_dim), lambda h: (0, 0, h)) for size in sizes]
        + [pl.BlockSpec((heads_step, 1, 128), lambda h: (h, 0, 0))],
        out_shape=[jax.ShapeDtypeStruct((3, size, width), jnp.bfloat16) for size in sizes]
        + [jax.ShapeDtypeStruct((heads, 1, 128), jnp.float32)],
        compiler_params=pltpu.CompilerParams(vmem_limit_bytes=VMEM_LIMIT),
        cost_estimate=pl.CostEstimate(
            flops=10 * length * length * width // SHADE,
            bytes_accessed=14 * length * width // SHADE,
            transcendentals=heads * length * length // SHADE,
        ),
        name="attention_back",
    )(key_bias, flags, queries, keys, values, grads)
    return outs[:-1], outs[-1][:, 0, 0]


def input_grad_body(count, place_ref, *refs):
    grad_refs, weight_refs, low_ref = refs[:count], refs[count:count + 3], refs[-1]
    out_refs = refs[count + 4:-1]
    me = place_ref[place_ref.shape[0] - 1]
    total = None
    for member in range(3):
        rows = jnp.concatenate([ref[member] for ref in grad_refs], axis=0)
        term = lax.dot_general(rows, weight_refs[member][...], NT, preferred_element_type=jnp.float32)
        total = term if total is None else total + term
    low_ref[...] = total.astype(jnp.bfloat16)
    begin = 0
    at = 0
    for ref in grad_refs:
        size = ref.shape[1] // len(out_refs)
        for apart, out_ref in enumerate(out_refs):
            out_ref[at:at + size, :] = low_ref[pl.ds(pl.multiple_of(begin + (me ^ apart) * size, 16), size), :]
        begin += ref.shape[1]
        at += size


def input_grad(place, grads, weights, pieces, ahead):
    rows_in, width = weights[0].shape
    tokens = sum(grad.shape[1] for grad in grads)
    step = 256
    return pl.pallas_call(
        functools.partial(input_grad_body, len(grads)),
        grid_spec=pltpu.PrefetchScalarGridSpec(
            num_scalar_prefetch=1,
            grid=(rows_in // step,),
            in_specs=[pl.BlockSpec(grad.shape, lambda n, place: (0, 0, 0)) for grad in grads]
            + [pl.BlockSpec((step, width), lambda n, place: (n, 0))] * 3
            + [pl.BlockSpec(memory_space=pl.ANY)],
            out_specs=[pl.BlockSpec((tokens // pieces, step), lambda n, place: (0, n))] * pieces,
            scratch_shapes=[pltpu.VMEM((tokens, step), jnp.bfloat16)],
        ),
        out_shape=[jax.ShapeDtypeStruct((tokens // pieces, rows_in), jnp.bfloat16)] * pieces,
        compiler_params=pltpu.CompilerParams(vmem_limit_bytes=8 * MIB + 14 * tokens * width + 12 * step * width),
        cost_estimate=pl.CostEstimate(
            flops=6 * tokens * rows_in * width // SHADE,
            bytes_accessed=6 * width * (rows_in + tokens) // SHADE,
            transcendentals=0,
        ),
        name="input_grad",
    )(place, *grads, *weights, ahead)


def weight_grad_body(pieces, units, has_acc, place_ref, *refs):
    count = len(units)
    x_refs, grad_refs = refs[:pieces], refs[pieces:pieces + count]
    acc_refs, out_refs, left_ref = refs[pieces + count:-4], refs[-4:-1], refs[-1]
    features = x_refs[0].shape[2]

    @pl.when(pl.program_id(0) == 0)
    def _():
        me = place_ref[place_ref.shape[0] - 1]
        for at, (hop, which, index) in enumerate(units):
            size = grad_refs[at].shape[1]
            for apart, x_ref in enumerate(x_refs):
                rows = pl.ds(pl.multiple_of((me ^ apart) * features, features), features)
                part = x_ref[place_ref[2 * hop + which], index * size:(index + 1) * size, :]
                left_ref[rows, at * size:(at + 1) * size] = part.T

    for member in range(3):
        right = jnp.concatenate([ref[member] for ref in grad_refs], axis=0)
        total = jnp.dot(left_ref[...], right, preferred_element_type=jnp.float32)
        if has_acc:
            total = total + acc_refs[member][...].astype(jnp.float32)
        out_refs[member][...] = total.astype(jnp.bfloat16)


def weight_grad(place, x, units, grads, acc):
    canvases, length, features = x[0].shape
    rows_in = len(x) * features
    size, width = grads[0].shape[1:]
    tokens = size * len(grads)
    step = min(width, 512 if len(grads) > 2 else 1024)
    block = pl.BlockSpec((rows_in, step), lambda n, place: (0, n))
    acc = tuple(acc) if acc is not None else ()
    return pl.pallas_call(
        functools.partial(weight_grad_body, len(x), tuple(units), bool(acc)),
        grid_spec=pltpu.PrefetchScalarGridSpec(
            num_scalar_prefetch=1,
            grid=(width // step,),
            in_specs=[pl.BlockSpec(x[0].shape, lambda n, place: (0, 0, 0))] * len(x)
            + [pl.BlockSpec((3, size, step), lambda n, place: (0, 0, n))] * len(grads)
            + [block] * len(acc),
            out_specs=[block] * 3,
            scratch_shapes=[pltpu.VMEM((rows_in, tokens), jnp.bfloat16)],
        ),
        out_shape=[jax.ShapeDtypeStruct((rows_in, width), jnp.bfloat16)] * 3,
        compiler_params=pltpu.CompilerParams(vmem_limit_bytes=12 * MIB + 12 * tokens * step + 4 * rows_in * tokens + rows_in * step * (32 if acc else 20)),
        cost_estimate=pl.CostEstimate(
            flops=6 * tokens * rows_in * width // SHADE,
            bytes_accessed=6 * width * (tokens + rows_in * (2 if acc else 1)) // SHADE,
            transcendentals=0,
        ),
        name="weight_grad",
    )(place, *x, *grads, *acc)


def sort_home_body(count, place_ref, *refs):
    part_refs, out_refs, held_ref = refs[:count], refs[count:-1], refs[-1]
    for step, ref in enumerate(part_refs):
        held_ref[2 * step:2 * step + 2] = ref[...]
    spread = out_refs[0].shape[0]
    for d, out_ref in enumerate(out_refs):
        for n in range(spread):
            out_ref[n] = held_ref[place_ref[2 * count + d * spread + n]]


def sort_home(place, parts, pieces, spread):
    _, tokens, rows_in = parts[0].shape
    return pl.pallas_call(
        functools.partial(sort_home_body, len(parts)),
        grid_spec=pltpu.PrefetchScalarGridSpec(
            num_scalar_prefetch=1,
            grid=(1,),
            in_specs=[pl.BlockSpec(part.shape, lambda n, place: (0, 0, 0)) for part in parts],
            out_specs=[pl.BlockSpec((spread, tokens, rows_in), lambda n, place: (0, 0, 0))] * pieces,
            scratch_shapes=[pltpu.VMEM((2 * len(parts), tokens, rows_in), jnp.bfloat16)],
        ),
        out_shape=[jax.ShapeDtypeStruct((spread, tokens, rows_in), jnp.bfloat16)] * pieces,
        compiler_params=pltpu.CompilerParams(vmem_limit_bytes=24 * MIB),
        cost_estimate=pl.CostEstimate(flops=0, bytes_accessed=4 * pieces * spread * tokens * rows_in, transcendentals=0),
        name="sort_home",
    )(place, *parts)


def assemble_body(count, sizes, place_ref, *refs):
    part_refs, out_ref = refs[:count], refs[count]
    me = place_ref[place_ref.shape[0] - 1]
    spread, _, rows_in = part_refs[0].shape
    begin = at = 0
    for whole in sizes:
        size = whole // count
        for d, ref in enumerate(part_refs):
            rows = pl.ds(pl.multiple_of(begin + (me ^ d) * size, 16), size)
            for n in range(spread):
                out_ref[rows, n * rows_in:(n + 1) * rows_in] = ref[n, at:at + size, :]
        begin += whole
        at += size


def assemble(place, parts, sizes):
    spread, tokens, rows_in = parts[0].shape
    return pl.pallas_call(
        functools.partial(assemble_body, len(parts), sizes),
        grid_spec=pltpu.PrefetchScalarGridSpec(
            num_scalar_prefetch=1,
            grid=(1,),
            in_specs=[pl.BlockSpec(part.shape, lambda n, place: (0, 0, 0)) for part in parts],
            out_specs=pl.BlockSpec((sum(sizes), spread * rows_in), lambda n, place: (0, 0)),
        ),
        out_shape=jax.ShapeDtypeStruct((sum(sizes), spread * rows_in), jnp.bfloat16),
        compiler_params=pltpu.CompilerParams(vmem_limit_bytes=24 * MIB),
        cost_estimate=pl.CostEstimate(
            flops=0, bytes_accessed=4 * len(parts) * spread * tokens * rows_in, transcendentals=0
        ),
        name="assemble",
    )(place, *parts)


def ring_order(chips):
    return [0] + list(range(1, chips, 2)) + list(range(chips - 2 + chips % 2, 0, -2))


def local(layer_input, attn_grad, queries, keys, values, masked, key_bias, w_query, w_key, w_value):
    row_count = lax.axis_size("row")
    col_count = lax.axis_size("col")
    length, width = queries.shape[1], queries.shape[2]
    rows_in = w_query.shape[0]
    spread = row_count // col_count
    chips = row_count // 2
    sizes = chunk_sizes(length)
    weights = (w_query, w_key, w_value)

    order = ring_order(chips)
    ring = [(2 * order[n] + core, 2 * order[(n + 1) % chips] + core) for n in range(chips) for core in range(2)]
    swap = [(n, n ^ 1) for n in range(row_count)]
    table = []
    for row in range(row_count):
        for col in range(col_count):
            at, core = order.index(row // 2), row % 2
            origin = [2 * order[(at - step) % chips] + (core ^ which) for step in range(chips) for which in range(2)]
            slot = [2 * ((order.index(r // 2) - at) % chips) + (r % 2 ^ core) for r in range(row_count)]
            slot = [slot[(col ^ d) * spread + n] for d in range(col_count) for n in range(spread)]
            table.append(origin + slot + [col])
    my_col = lax.axis_index("col")
    place = jnp.array(table, jnp.int32)[lax.axis_index("row") * col_count + my_col]

    def a2a(array, axis):
        return lax.all_to_all(array, axis, split_axis=0, concat_axis=0, tiled=True)

    def after(array, ahead):
        return lax.optimization_barrier((array, ahead))[0]

    always = jnp.sum(masked) >= 0

    def window(work, *operands):
        shapes = jax.eval_shape(work, *operands)

        def nothing(*_):
            return jax.tree.map(lambda leaf: jnp.zeros(leaf.shape, leaf.dtype), shapes)

        return lax.cond(always, work, nothing, *operands)

    every = range(len(sizes))
    last, final = len(sizes) - 1, chips - 1

    def hop(mine):
        return lax.ppermute(mine, "row", ring)

    def other(mine):
        return lax.ppermute(mine, "row", swap)

    def across(mine, apart):
        return lax.ppermute(mine, "col", [(n, n ^ apart) for n in range(col_count)])

    def partial_of(given, ahead=None):
        ahead = given[-1][1] if ahead is None else ahead
        return input_grad(place, [member for pair in given for member in pair], weights, col_count, ahead)

    def summed(partial, beside=()):
        parts = after([across(partial[d], d) if d else partial[d] for d in range(col_count)], beside)
        return sum(part.astype(jnp.float32) for part in parts).astype(jnp.bfloat16)

    def shared(total, chunks_in):
        mine, theirs = [], []
        at = 0
        for size in chunks_in:
            size = size // col_count
            mine.append(total[at:at + size])
            theirs.append(total[at + size:at + 2 * size])
            at += 2 * size
        return jnp.stack([jnp.concatenate(mine, axis=0), other(jnp.concatenate(theirs, axis=0))])

    def weight_part(x, units, given, acc):
        places = [(step, core, index) for step, index in units for core in range(2)]
        return weight_grad(place, x, places, [member for pair in given for member in pair], acc)

    chunks, bias_part = attention(queries[0], keys[0], values[0], attn_grad, masked, key_bias, sizes)
    arrived = [list(chunks)] + [[None] * len(sizes) for _ in range(final)]
    others = [[None] * len(sizes) for _ in range(chips)]
    sums = [None] * chips

    def both(step, index):
        return (arrived[step][index], others[step][index])

    def own_tokens(layer_input, *chunks):
        blocks = layer_input.reshape(length, spread, col_count, rows_in // col_count)
        x = a2a(jnp.transpose(blocks, (2, 1, 0, 3)), "col").reshape(row_count, length, rows_in // col_count)
        theirs = [other(chunk) for chunk in chunks]
        partial = partial_of(list(zip(chunks, theirs)))
        x = a2a(after(x, partial[0]), "row")
        return theirs, shared(summed(partial), sizes), x

    arrived[1][0] = hop(chunks[0])
    others[0], sums[0], x = window(own_tokens, layer_input, *chunks)
    arrived[1][last] = hop(after(chunks[last], others[0][0]))
    x_pieces = {0: x}

    weight_grads = None
    for step in range(1, final):
        units = [(place, spot) for place in range(2) for spot in every] if step == 2 else []

        def early(mine, x, done, partial):
            theirs = other(mine)
            if step == 1:
                return theirs, [across(x, apart) for apart in range(1, col_count) if apart & (apart - 1) == 0]
            if step == 2:
                acc = weight_part(x, units, done, None)
                return theirs, shared(summed(partial, acc[0]), sizes), acc
            return theirs, shared(partial, sizes)

        others[step][0], *given = window(early, arrived[step][0], x, [both(*unit) for unit in units], sums[step - 1])
        if step == 1:
            x_pieces.update(zip([apart for apart in range(1, col_count) if apart & (apart - 1) == 0], given[0]))
        elif step == 2:
            sums[1], weight_grads = given
        else:
            (sums[step - 1],) = given
        arrived[step + 1][0] = hop(after(arrived[step][0], others[step][0]))

        def late(mine, x, sooner, acc):
            theirs = other(mine)
            given = [sooner, (mine, theirs)]
            partial = partial_of(given)
            if step == 1:
                return theirs, partial, [across(x, apart) for apart in range(1, col_count) if apart & (apart - 1)]
            acc = weight_part(x, [(step, spot) for spot in every], given, acc)
            return theirs, summed(partial, acc[0]), acc

        others[step][last], sums[step], given = window(late, arrived[step][last], x, both(step, 0), weight_grads)
        if step == 1:
            x_pieces.update(zip([apart for apart in range(1, col_count) if apart & (apart - 1)], given))
            x = [x_pieces[apart] for apart in range(col_count)]
        else:
            weight_grads = given
        arrived[step + 1][last] = hop(after(arrived[step][last], others[step][last]))

    def before_last(mine, x, acc, total):
        theirs = other(mine)
        given = [(mine, theirs)]
        partial = partial_of(given)
        acc = weight_part(x, [(final, 0)], given, acc)
        return theirs, shared(summed(partial, acc[0]), sizes[:last]), acc, shared(total, sizes)

    others[final][0], sooner, weight_grads, sums[final - 1] = window(
        before_last, after(arrived[final][0], others[final - 1][last]), x, weight_grads, sums[final - 1]
    )

    def homeward(mine, step):
        route = [(2 * order[n] + core, 2 * order[(n - step) % chips] + core) for n in range(chips) for core in range(2)]
        return lax.ppermute(mine, "row", route) if step else mine

    landed = after(arrived[final][last], others[final][0])
    others[final][last] = other(landed)
    sums, sooner = after((sums, sooner), landed)
    at_home = [homeward(sums[step], step) for step in range(final)]
    partial = partial_of([(landed, others[final][last])], others[final][0])

    def folded(bias, bit, ahead):
        bias = after(bias, ahead)
        return bias + lax.ppermute(bias, "row", [(n, n ^ 1 << bit) for n in range(row_count)])

    bias_grad = folded(bias_part, 0, landed)
    total = summed(partial, (at_home, bias_grad))
    sooner = homeward(jnp.concatenate([sooner, shared(total, sizes[last:])], axis=1), final)
    weight_grads = weight_part(after(x, total), [(final, last)], [both(final, last)], weight_grads)
    at_home.append(after(sooner, weight_grads[0]))
    mine = sort_home(place, at_home, col_count, spread)
    got = [across(mine[d], d) if d else mine[d] for d in range(col_count)]
    for bit in range(1, row_count.bit_length() - 1):
        bias_grad = folded(bias_grad, bit, mine[0])
    layer_grad = assemble(place, after(got, bias_grad), sizes)
    return (layer_grad, *weight_grads, bias_grad)


def solution(mesh):
    in_specs = (
        P("row", "col"),
        P("row", "col"),
        P("row", None, "col"),
        P("row", None, "col"),
        P("row", None, "col"),
        P("row", None),
        P("col"),
        P("row", "col"),
        P("row", "col"),
        P("row", "col"),
    )
    out_specs = (P("row", "col"), P("row", "col"), P("row", "col"), P("row", "col"), P("col"))
    return jax.shard_map(local, mesh=mesh, in_specs=in_specs, out_specs=out_specs, check_vma=False)
```

```python
import functools
import math

import jax
import jax.numpy as jnp
from jax import lax
from jax.experimental import pallas as pl
from jax.experimental.pallas import tpu as pltpu
from jax.sharding import PartitionSpec as P

NT = (((1,), (1,)), ((), ()))
TN = (((0,), (0,)), ((), ()))
MIB = 1024 * 1024
VMEM_LIMIT = 56 * MIB
SHADE = 20


def chunk_sizes(length):
    return (length // 2, length - length // 2)


def attention_body(sizes, head_dim, heads_step, bias_ref, flag_ref, q_ref, k_ref, v_ref, g_ref, *outs):
    chunk_refs, bias_out = outs[:-1], outs[-1]
    scale_qk = 1.0 / math.sqrt(head_dim)
    flag = flag_ref[...].astype(jnp.float32)
    for sub in range(heads_step):
        cols = slice(sub * head_dim, (sub + 1) * head_dim)
        q, k, v, g = q_ref[:, cols], k_ref[:, cols], v_ref[:, cols], g_ref[:, cols]
        head = pl.program_id(0) * heads_step + sub
        scores = lax.dot_general(q, k, NT, preferred_element_type=jnp.float32) * scale_qk + bias_ref[head] * flag
        exp_terms = jnp.exp(scores - jnp.max(scores, axis=-1, keepdims=True))
        probs = exp_terms * (1.0 / jnp.sum(exp_terms, axis=-1, keepdims=True))
        probs_low = probs.astype(jnp.bfloat16)
        grad_probs = lax.dot_general(g, v, NT, preferred_element_type=jnp.float32)
        delta = jnp.sum(probs_low.astype(jnp.float32) * grad_probs, axis=-1, keepdims=True)
        grad_scores = probs * (grad_probs - delta)
        grad_low = grad_scores.astype(jnp.bfloat16)
        value_grad = lax.dot_general(probs_low, g, TN, preferred_element_type=jnp.float32)
        query_grad = jnp.dot(grad_low, k, preferred_element_type=jnp.float32) * scale_qk
        key_grad = lax.dot_general(grad_low, q, TN, preferred_element_type=jnp.float32) * scale_qk
        bias = jnp.sum(jnp.sum(grad_scores, axis=0, keepdims=True) * flag, axis=1, keepdims=True)
        bias_out[sub] = jnp.broadcast_to(bias, (1, 128))
        for place, member in enumerate((query_grad, key_grad, value_grad)):
            low = member.astype(jnp.bfloat16)
            begin = 0
            for size, ref in zip(sizes, chunk_refs):
                ref[place, :, cols] = low[begin:begin + size]
                begin += size


def attention(queries, keys, values, grads, flags, key_bias, sizes):
    length, width = queries.shape
    heads = key_bias.shape[0]
    head_dim = width // heads
    heads_step = math.gcd(heads, 4)
    block = pl.BlockSpec((length, heads_step * head_dim), lambda h: (0, h))
    outs = pl.pallas_call(
        functools.partial(attention_body, sizes, head_dim, heads_step),
        grid=(heads // heads_step,),
        in_specs=[
            pl.BlockSpec(memory_space=pltpu.SMEM),
            pl.BlockSpec((1, length), lambda h: (0, 0)),
            block, block, block, block,
        ],
        out_specs=[pl.BlockSpec((3, size, heads_step * head_dim), lambda h: (0, 0, h)) for size in sizes]
        + [pl.BlockSpec((heads_step, 1, 128), lambda h: (h, 0, 0))],
        out_shape=[jax.ShapeDtypeStruct((3, size, width), jnp.bfloat16) for size in sizes]
        + [jax.ShapeDtypeStruct((heads, 1, 128), jnp.float32)],
        compiler_params=pltpu.CompilerParams(vmem_limit_bytes=VMEM_LIMIT),
        cost_estimate=pl.CostEstimate(
            flops=10 * length * length * width // SHADE,
            bytes_accessed=14 * length * width // SHADE,
            transcendentals=heads * length * length // SHADE,
        ),
        name="attention_back",
    )(key_bias, flags, queries, keys, values, grads)
    return outs[:-1], outs[-1][:, 0, 0]


def input_grad_body(count, place_ref, *refs):
    grad_refs, weight_refs, low_ref = refs[:count], refs[count:count + 3], refs[-1]
    out_refs = refs[count + 4:-1]
    me = place_ref[place_ref.shape[0] - 1]
    total = None
    for member in range(3):
        rows = jnp.concatenate([ref[member] for ref in grad_refs], axis=0)
        term = lax.dot_general(rows, weight_refs[member][...], NT, preferred_element_type=jnp.float32)
        total = term if total is None else total + term
    low_ref[...] = total.astype(jnp.bfloat16)
    begin = 0
    at = 0
    for ref in grad_refs:
        size = ref.shape[1] // len(out_refs)
        for apart, out_ref in enumerate(out_refs):
            out_ref[at:at + size, :] = low_ref[pl.ds(pl.multiple_of(begin + (me ^ apart) * size, 16), size), :]
        begin += ref.shape[1]
        at += size


def input_grad(place, grads, weights, pieces, ahead):
    rows_in, width = weights[0].shape
    tokens = sum(grad.shape[1] for grad in grads)
    step = 256
    return pl.pallas_call(
        functools.partial(input_grad_body, len(grads)),
        grid_spec=pltpu.PrefetchScalarGridSpec(
            num_scalar_prefetch=1,
            grid=(rows_in // step,),
            in_specs=[pl.BlockSpec(grad.shape, lambda n, place: (0, 0, 0)) for grad in grads]
            + [pl.BlockSpec((step, width), lambda n, place: (n, 0))] * 3
            + [pl.BlockSpec(memory_space=pl.ANY)],
            out_specs=[pl.BlockSpec((tokens // pieces, step), lambda n, place: (0, n))] * pieces,
            scratch_shapes=[pltpu.VMEM((tokens, step), jnp.bfloat16)],
        ),
        out_shape=[jax.ShapeDtypeStruct((tokens // pieces, rows_in), jnp.bfloat16)] * pieces,
        compiler_params=pltpu.CompilerParams(vmem_limit_bytes=8 * MIB + 14 * tokens * width + 12 * step * width),
        cost_estimate=pl.CostEstimate(
            flops=6 * tokens * rows_in * width // SHADE,
            bytes_accessed=6 * width * (rows_in + tokens) // SHADE,
            transcendentals=0,
        ),
        name="input_grad",
    )(place, *grads, *weights, ahead)


def weight_grad_body(pieces, units, has_acc, place_ref, *refs):
    count = len(units)
    x_refs, grad_refs = refs[:pieces], refs[pieces:pieces + count]
    acc_refs, out_refs, left_ref = refs[pieces + count:-4], refs[-4:-1], refs[-1]
    features = x_refs[0].shape[2]

    @pl.when(pl.program_id(0) == 0)
    def _():
        me = place_ref[place_ref.shape[0] - 1]
        for at, (hop, which, index) in enumerate(units):
            size = grad_refs[at].shape[1]
            for apart, x_ref in enumerate(x_refs):
                rows = pl.ds(pl.multiple_of((me ^ apart) * features, features), features)
                part = x_ref[place_ref[2 * hop + which], index * size:(index + 1) * size, :]
                left_ref[rows, at * size:(at + 1) * size] = part.T

    for member in range(3):
        right = jnp.concatenate([ref[member] for ref in grad_refs], axis=0)
        total = jnp.dot(left_ref[...], right, preferred_element_type=jnp.float32)
        if has_acc:
            total = total + acc_refs[member][...].astype(jnp.float32)
        out_refs[member][...] = total.astype(jnp.bfloat16)


def weight_grad(place, x, units, grads, acc):
    canvases, length, features = x[0].shape
    rows_in = len(x) * features
    size, width = grads[0].shape[1:]
    tokens = size * len(grads)
    step = min(width, 512 if len(grads) > 2 else 1024)
    block = pl.BlockSpec((rows_in, step), lambda n, place: (0, n))
    acc = tuple(acc) if acc is not None else ()
    return pl.pallas_call(
        functools.partial(weight_grad_body, len(x), tuple(units), bool(acc)),
        grid_spec=pltpu.PrefetchScalarGridSpec(
            num_scalar_prefetch=1,
            grid=(width // step,),
            in_specs=[pl.BlockSpec(x[0].shape, lambda n, place: (0, 0, 0))] * len(x)
            + [pl.BlockSpec((3, size, step), lambda n, place: (0, 0, n))] * len(grads)
            + [block] * len(acc),
            out_specs=[block] * 3,
            scratch_shapes=[pltpu.VMEM((rows_in, tokens), jnp.bfloat16)],
        ),
        out_shape=[jax.ShapeDtypeStruct((rows_in, width), jnp.bfloat16)] * 3,
        compiler_params=pltpu.CompilerParams(vmem_limit_bytes=12 * MIB + 12 * tokens * step + 4 * rows_in * tokens + rows_in * step * (32 if acc else 20)),
        cost_estimate=pl.CostEstimate(
            flops=6 * tokens * rows_in * width // SHADE,
            bytes_accessed=6 * width * (tokens + rows_in * (2 if acc else 1)) // SHADE,
            transcendentals=0,
        ),
        name="weight_grad",
    )(place, *x, *grads, *acc)


def sort_home_body(count, place_ref, *refs):
    part_refs, out_refs, held_ref = refs[:count], refs[count:-1], refs[-1]
    for step, ref in enumerate(part_refs):
        held_ref[2 * step:2 * step + 2] = ref[...]
    spread = out_refs[0].shape[0]
    for d, out_ref in enumerate(out_refs):
        for n in range(spread):
            out_ref[n] = held_ref[place_ref[2 * count + d * spread + n]]


def sort_home(place, parts, pieces, spread):
    _, tokens, rows_in = parts[0].shape
    return pl.pallas_call(
        functools.partial(sort_home_body, len(parts)),
        grid_spec=pltpu.PrefetchScalarGridSpec(
            num_scalar_prefetch=1,
            grid=(1,),
            in_specs=[pl.BlockSpec(part.shape, lambda n, place: (0, 0, 0)) for part in parts],
            out_specs=[pl.BlockSpec((spread, tokens, rows_in), lambda n, place: (0, 0, 0))] * pieces,
            scratch_shapes=[pltpu.VMEM((2 * len(parts), tokens, rows_in), jnp.bfloat16)],
        ),
        out_shape=[jax.ShapeDtypeStruct((spread, tokens, rows_in), jnp.bfloat16)] * pieces,
        compiler_params=pltpu.CompilerParams(vmem_limit_bytes=24 * MIB),
        cost_estimate=pl.CostEstimate(flops=0, bytes_accessed=4 * pieces * spread * tokens * rows_in, transcendentals=0),
        name="sort_home",
    )(place, *parts)


def assemble_body(count, sizes, place_ref, *refs):
    part_refs, out_ref = refs[:count], refs[count]
    me = place_ref[place_ref.shape[0] - 1]
    spread, _, rows_in = part_refs[0].shape
    begin = at = 0
    for whole in sizes:
        size = whole // count
        for d, ref in enumerate(part_refs):
            rows = pl.ds(pl.multiple_of(begin + (me ^ d) * size, 16), size)
            for n in range(spread):
                out_ref[rows, n * rows_in:(n + 1) * rows_in] = ref[n, at:at + size, :]
        begin += whole
        at += size


def assemble(place, parts, sizes):
    spread, tokens, rows_in = parts[0].shape
    return pl.pallas_call(
        functools.partial(assemble_body, len(parts), sizes),
        grid_spec=pltpu.PrefetchScalarGridSpec(
            num_scalar_prefetch=1,
            grid=(1,),
            in_specs=[pl.BlockSpec(part.shape, lambda n, place: (0, 0, 0)) for part in parts],
            out_specs=pl.BlockSpec((sum(sizes), spread * rows_in), lambda n, place: (0, 0)),
        ),
        out_shape=jax.ShapeDtypeStruct((sum(sizes), spread * rows_in), jnp.bfloat16),
        compiler_params=pltpu.CompilerParams(vmem_limit_bytes=24 * MIB),
        cost_estimate=pl.CostEstimate(
            flops=0, bytes_accessed=4 * len(parts) * spread * tokens * rows_in, transcendentals=0
        ),
        name="assemble",
    )(place, *parts)


def ring_order(chips):
    return [0] + list(range(1, chips, 2)) + list(range(chips - 2 + chips % 2, 0, -2))


def local(layer_input, attn_grad, queries, keys, values, masked, key_bias, w_query, w_key, w_value):
    row_count = lax.axis_size("row")
    col_count = lax.axis_size("col")
    length, width = queries.shape[1], queries.shape[2]
    rows_in = w_query.shape[0]
    spread = row_count // col_count
    chips = row_count // 2
    sizes = chunk_sizes(length)
    weights = (w_query, w_key, w_value)

    order = ring_order(chips)
    ring = [(2 * order[n] + core, 2 * order[(n + 1) % chips] + core) for n in range(chips) for core in range(2)]
    swap = [(n, n ^ 1) for n in range(row_count)]
    table = []
    for row in range(row_count):
        for col in range(col_count):
            at, core = order.index(row // 2), row % 2
            origin = [2 * order[(at - step) % chips] + (core ^ which) for step in range(chips) for which in range(2)]
            slot = [2 * ((order.index(r // 2) - at) % chips) + (r % 2 ^ core) for r in range(row_count)]
            slot = [slot[(col ^ d) * spread + n] for d in range(col_count) for n in range(spread)]
            table.append(origin + slot + [col])
    my_col = lax.axis_index("col")
    place = jnp.array(table, jnp.int32)[lax.axis_index("row") * col_count + my_col]

    def a2a(array, axis):
        return lax.all_to_all(array, axis, split_axis=0, concat_axis=0, tiled=True)

    def after(array, ahead):
        return lax.optimization_barrier((array, ahead))[0]

    always = jnp.sum(masked) >= 0

    def window(work, *operands):
        shapes = jax.eval_shape(work, *operands)

        def nothing(*_):
            return jax.tree.map(lambda leaf: jnp.zeros(leaf.shape, leaf.dtype), shapes)

        return lax.cond(always, work, nothing, *operands)

    every = range(len(sizes))
    last, final = len(sizes) - 1, chips - 1

    def hop(mine):
        return lax.ppermute(mine, "row", ring)

    def other(mine):
        return lax.ppermute(mine, "row", swap)

    def across(mine, apart):
        return lax.ppermute(mine, "col", [(n, n ^ apart) for n in range(col_count)])

    def partial_of(given, ahead=None):
        ahead = given[-1][1] if ahead is None else ahead
        return input_grad(place, [member for pair in given for member in pair], weights, col_count, ahead)

    def summed(partial, beside=()):
        parts = after([across(partial[d], d) if d else partial[d] for d in range(col_count)], beside)
        return sum(part.astype(jnp.float32) for part in parts).astype(jnp.bfloat16)

    def shared(total, chunks_in):
        mine, theirs = [], []
        at = 0
        for size in chunks_in:
            size = size // col_count
            mine.append(total[at:at + size])
            theirs.append(total[at + size:at + 2 * size])
            at += 2 * size
        return jnp.stack([jnp.concatenate(mine, axis=0), other(jnp.concatenate(theirs, axis=0))])

    def weight_part(x, units, given, acc):
        places = [(step, core, index) for step, index in units for core in range(2)]
        return weight_grad(place, x, places, [member for pair in given for member in pair], acc)

    chunks, bias_part = attention(queries[0], keys[0], values[0], attn_grad, masked, key_bias, sizes)
    arrived = [list(chunks)] + [[None] * len(sizes) for _ in range(final)]
    others = [[None] * len(sizes) for _ in range(chips)]
    sums = [None] * chips

    def both(step, index):
        return (arrived[step][index], others[step][index])

    def own_tokens(layer_input, *chunks):
        blocks = layer_input.reshape(length, spread, col_count, rows_in // col_count)
        x = a2a(jnp.transpose(blocks, (2, 1, 0, 3)), "col").reshape(row_count, length, rows_in // col_count)
        theirs = [other(chunk) for chunk in chunks]
        partial = partial_of(list(zip(chunks, theirs)))
        x = a2a(after(x, partial[0]), "row")
        return theirs, shared(summed(partial), sizes), x

    arrived[1][0] = hop(chunks[0])
    others[0], sums[0], x = window(own_tokens, layer_input, *chunks)
    arrived[1][last] = hop(after(chunks[last], others[0][0]))
    x_pieces = {0: x}

    weight_grads = None
    for step in range(1, final):
        units = [(place, spot) for place in range(2) for spot in every] if step == 2 else []

        def early(mine, x, done, partial):
            theirs = other(mine)
            if step == 1:
                return theirs, [across(x, apart) for apart in range(1, col_count) if apart & (apart - 1) == 0]
            if step == 2:
                acc = weight_part(x, units, done, None)
                return theirs, shared(summed(partial, acc[0]), sizes), acc
            return theirs, shared(partial, sizes)

        others[step][0], *given = window(early, arrived[step][0], x, [both(*unit) for unit in units], sums[step - 1])
        if step == 1:
            x_pieces.update(zip([apart for apart in range(1, col_count) if apart & (apart - 1) == 0], given[0]))
        elif step == 2:
            sums[1], weight_grads = given
        else:
            (sums[step - 1],) = given
        arrived[step + 1][0] = hop(after(arrived[step][0], others[step][0]))

        def late(mine, x, sooner, acc):
            theirs = other(mine)
            given = [sooner, (mine, theirs)]
            partial = partial_of(given)
            if step == 1:
                return theirs, partial, [across(x, apart) for apart in range(1, col_count) if apart & (apart - 1)]
            acc = weight_part(x, [(step, spot) for spot in every], given, acc)
            return theirs, summed(partial, acc[0]), acc

        others[step][last], sums[step], given = window(late, arrived[step][last], x, both(step, 0), weight_grads)
        if step == 1:
            x_pieces.update(zip([apart for apart in range(1, col_count) if apart & (apart - 1)], given))
            x = [x_pieces[apart] for apart in range(col_count)]
        else:
            weight_grads = given
        arrived[step + 1][last] = hop(after(arrived[step][last], others[step][last]))

    def before_last(mine, x, acc, total):
        theirs = other(mine)
        given = [(mine, theirs)]
        partial = partial_of(given)
        acc = weight_part(x, [(final, 0)], given, acc)
        return theirs, shared(summed(partial, acc[0]), sizes[:last]), acc, shared(total, sizes)

    others[final][0], sooner, weight_grads, sums[final - 1] = window(
        before_last, after(arrived[final][0], others[final - 1][last]), x, weight_grads, sums[final - 1]
    )

    def homeward(mine, step):
        route = [(2 * order[n] + core, 2 * order[(n - step) % chips] + core) for n in range(chips) for core in range(2)]
        return lax.ppermute(mine, "row", route) if step else mine

    landed = after(arrived[final][last], others[final][0])
    others[final][last] = other(landed)
    sums, sooner = after((sums, sooner), landed)
    at_home = [homeward(sums[step], step) for step in range(final)]
    partial = partial_of([(landed, others[final][last])], others[final][0])

    def folded(bias, bit, ahead):
        bias = after(bias, ahead)
        return bias + lax.ppermute(bias, "row", [(n, n ^ 1 << bit) for n in range(row_count)])

    bias_grad = folded(bias_part, 0, landed)
    total = summed(partial, (at_home, bias_grad))
    sooner = homeward(jnp.concatenate([sooner, shared(total, sizes[last:])], axis=1), final)
    for bit in range(1, row_count.bit_length() - 1):
        bias_grad = folded(bias_grad, bit, total)
    at_home.append(after(sooner, bias_grad))
    mine = sort_home(place, at_home, col_count, spread)
    got = [across(mine[d], d) if d else mine[d] for d in range(col_count)]
    weight_grads = weight_part(after(x, mine), [(final, last)], [both(final, last)], weight_grads)
    layer_grad = assemble(place, after(got, weight_grads[0]), sizes)
    return (layer_grad, *weight_grads, bias_grad)


def solution(mesh):
    in_specs = (
        P("row", "col"),
        P("row", "col"),
        P("row", None, "col"),
        P("row", None, "col"),
        P("row", None, "col"),
        P("row", None),
        P("col"),
        P("row", "col"),
        P("row", "col"),
        P("row", "col"),
    )
    out_specs = (P("row", "col"), P("row", "col"), P("row", "col"), P("row", "col"), P("col"))
    return jax.shard_map(local, mesh=mesh, in_specs=in_specs, out_specs=out_specs, check_vma=False)
```

```python
import functools
import math

import jax
import jax.numpy as jnp
from jax import lax
from jax.experimental import pallas as pl
from jax.experimental.pallas import tpu as pltpu
from jax.sharding import PartitionSpec as P

NT = (((1,), (1,)), ((), ()))
TN = (((0,), (0,)), ((), ()))
MIB = 1024 * 1024
VMEM_LIMIT = 56 * MIB
SHADE = 20


def chunk_sizes(length):
    return (length // 2, length - length // 2)


def attention_body(sizes, head_dim, heads_step, bias_ref, flag_ref, q_ref, k_ref, v_ref, g_ref, *outs):
    chunk_refs, bias_out = outs[:-1], outs[-1]
    scale_qk = 1.0 / math.sqrt(head_dim)
    flag = flag_ref[...].astype(jnp.float32)
    for sub in range(heads_step):
        cols = slice(sub * head_dim, (sub + 1) * head_dim)
        q, k, v, g = q_ref[:, cols], k_ref[:, cols], v_ref[:, cols], g_ref[:, cols]
        head = pl.program_id(0) * heads_step + sub
        scores = lax.dot_general(q, k, NT, preferred_element_type=jnp.float32) * scale_qk + bias_ref[head] * flag
        exp_terms = jnp.exp(scores - jnp.max(scores, axis=-1, keepdims=True))
        probs = exp_terms * (1.0 / jnp.sum(exp_terms, axis=-1, keepdims=True))
        probs_low = probs.astype(jnp.bfloat16)
        grad_probs = lax.dot_general(g, v, NT, preferred_element_type=jnp.float32)
        delta = jnp.sum(probs_low.astype(jnp.float32) * grad_probs, axis=-1, keepdims=True)
        grad_scores = probs * (grad_probs - delta)
        grad_low = grad_scores.astype(jnp.bfloat16)
        value_grad = lax.dot_general(probs_low, g, TN, preferred_element_type=jnp.float32)
        query_grad = jnp.dot(grad_low, k, preferred_element_type=jnp.float32) * scale_qk
        key_grad = lax.dot_general(grad_low, q, TN, preferred_element_type=jnp.float32) * scale_qk
        bias = jnp.sum(jnp.sum(grad_scores, axis=0, keepdims=True) * flag, axis=1, keepdims=True)
        bias_out[sub] = jnp.broadcast_to(bias, (1, 128))
        for place, member in enumerate((query_grad, key_grad, value_grad)):
            low = member.astype(jnp.bfloat16)
            begin = 0
            for size, ref in zip(sizes, chunk_refs):
                ref[place, :, cols] = low[begin:begin + size]
                begin += size


def attention(queries, keys, values, grads, flags, key_bias, sizes):
    length, width = queries.shape
    heads = key_bias.shape[0]
    head_dim = width // heads
    heads_step = math.gcd(heads, 4)
    block = pl.BlockSpec((length, heads_step * head_dim), lambda h: (0, h))
    outs = pl.pallas_call(
        functools.partial(attention_body, sizes, head_dim, heads_step),
        grid=(heads // heads_step,),
        in_specs=[
            pl.BlockSpec(memory_space=pltpu.SMEM),
            pl.BlockSpec((1, length), lambda h: (0, 0)),
            block, block, block, block,
        ],
        out_specs=[pl.BlockSpec((3, size, heads_step * head_dim), lambda h: (0, 0, h)) for size in sizes]
        + [pl.BlockSpec((heads_step, 1, 128), lambda h: (h, 0, 0))],
        out_shape=[jax.ShapeDtypeStruct((3, size, width), jnp.bfloat16) for size in sizes]
        + [jax.ShapeDtypeStruct((heads, 1, 128), jnp.float32)],
        compiler_params=pltpu.CompilerParams(vmem_limit_bytes=VMEM_LIMIT),
        cost_estimate=pl.CostEstimate(
            flops=10 * length * length * width // SHADE,
            bytes_accessed=14 * length * width // SHADE,
            transcendentals=heads * length * length // SHADE,
        ),
        name="attention_back",
    )(key_bias, flags, queries, keys, values, grads)
    return outs[:-1], outs[-1][:, 0, 0]


def input_grad_body(count, place_ref, *refs):
    grad_refs, weight_refs, low_ref = refs[:count], refs[count:count + 3], refs[-1]
    out_refs = refs[count + 4:-1]
    me = place_ref[place_ref.shape[0] - 1]
    total = None
    for member in range(3):
        rows = jnp.concatenate([ref[member] for ref in grad_refs], axis=0)
        term = lax.dot_general(rows, weight_refs[member][...], NT, preferred_element_type=jnp.float32)
        total = term if total is None else total + term
    low_ref[...] = total.astype(jnp.bfloat16)
    begin = 0
    at = 0
    for ref in grad_refs:
        size = ref.shape[1] // len(out_refs)
        for apart, out_ref in enumerate(out_refs):
            out_ref[at:at + size, :] = low_ref[pl.ds(pl.multiple_of(begin + (me ^ apart) * size, 16), size), :]
        begin += ref.shape[1]
        at += size


def input_grad(place, grads, weights, pieces, ahead):
    rows_in, width = weights[0].shape
    tokens = sum(grad.shape[1] for grad in grads)
    step = min(rows_in, 512 if len(grads) <= 2 else 256)
    return pl.pallas_call(
        functools.partial(input_grad_body, len(grads)),
        grid_spec=pltpu.PrefetchScalarGridSpec(
            num_scalar_prefetch=1,
            grid=(rows_in // step,),
            in_specs=[pl.BlockSpec(grad.shape, lambda n, place: (0, 0, 0)) for grad in grads]
            + [pl.BlockSpec((step, width), lambda n, place: (n, 0))] * 3
            + [pl.BlockSpec(memory_space=pl.ANY)],
            out_specs=[pl.BlockSpec((tokens // pieces, step), lambda n, place: (0, n))] * pieces,
            scratch_shapes=[pltpu.VMEM((tokens, step), jnp.bfloat16)],
        ),
        out_shape=[jax.ShapeDtypeStruct((tokens // pieces, rows_in), jnp.bfloat16)] * pieces,
        compiler_params=pltpu.CompilerParams(vmem_limit_bytes=8 * MIB + 14 * tokens * width + 12 * step * width),
        cost_estimate=pl.CostEstimate(
            flops=6 * tokens * rows_in * width // SHADE,
            bytes_accessed=6 * width * (rows_in + tokens) // SHADE,
            transcendentals=0,
        ),
        name="input_grad",
    )(place, *grads, *weights, ahead)


def weight_grad_body(pieces, units, has_acc, place_ref, *refs):
    count = len(units)
    x_refs, grad_refs = refs[:pieces], refs[pieces:pieces + count]
    acc_refs, out_refs, left_ref = refs[pieces + count:-4], refs[-4:-1], refs[-1]
    features = x_refs[0].shape[2]

    @pl.when(pl.program_id(0) == 0)
    def _():
        me = place_ref[place_ref.shape[0] - 1]
        for at, (hop, which, index) in enumerate(units):
            size = grad_refs[at].shape[1]
            for apart, x_ref in enumerate(x_refs):
                rows = pl.ds(pl.multiple_of((me ^ apart) * features, features), features)
                part = x_ref[place_ref[2 * hop + which], index * size:(index + 1) * size, :]
                left_ref[rows, at * size:(at + 1) * size] = part.T

    for member in range(3):
        right = jnp.concatenate([ref[member] for ref in grad_refs], axis=0)
        total = jnp.dot(left_ref[...], right, preferred_element_type=jnp.float32)
        if has_acc:
            total = total + acc_refs[member][...].astype(jnp.float32)
        out_refs[member][...] = total.astype(jnp.bfloat16)


def weight_grad(place, x, units, grads, acc):
    canvases, length, features = x[0].shape
    rows_in = len(x) * features
    size, width = grads[0].shape[1:]
    tokens = size * len(grads)
    step = min(width, 512 if len(grads) > 2 else 1024)
    block = pl.BlockSpec((rows_in, step), lambda n, place: (0, n))
    acc = tuple(acc) if acc is not None else ()
    return pl.pallas_call(
        functools.partial(weight_grad_body, len(x), tuple(units), bool(acc)),
        grid_spec=pltpu.PrefetchScalarGridSpec(
            num_scalar_prefetch=1,
            grid=(width // step,),
            in_specs=[pl.BlockSpec(x[0].shape, lambda n, place: (0, 0, 0))] * len(x)
            + [pl.BlockSpec((3, size, step), lambda n, place: (0, 0, n))] * len(grads)
            + [block] * len(acc),
            out_specs=[block] * 3,
            scratch_shapes=[pltpu.VMEM((rows_in, tokens), jnp.bfloat16)],
        ),
        out_shape=[jax.ShapeDtypeStruct((rows_in, width), jnp.bfloat16)] * 3,
        compiler_params=pltpu.CompilerParams(vmem_limit_bytes=12 * MIB + 12 * tokens * step + 4 * rows_in * tokens + rows_in * step * (32 if acc else 20)),
        cost_estimate=pl.CostEstimate(
            flops=6 * tokens * rows_in * width // SHADE,
            bytes_accessed=6 * width * (tokens + rows_in * (2 if acc else 1)) // SHADE,
            transcendentals=0,
        ),
        name="weight_grad",
    )(place, *x, *grads, *acc)


def sort_home_body(count, place_ref, *refs):
    part_refs, out_refs, held_ref = refs[:count], refs[count:-1], refs[-1]
    for step, ref in enumerate(part_refs):
        held_ref[2 * step:2 * step + 2] = ref[...]
    spread = out_refs[0].shape[0]
    for d, out_ref in enumerate(out_refs):
        for n in range(spread):
            out_ref[n] = held_ref[place_ref[2 * count + d * spread + n]]


def sort_home(place, parts, pieces, spread):
    _, tokens, rows_in = parts[0].shape
    return pl.pallas_call(
        functools.partial(sort_home_body, len(parts)),
        grid_spec=pltpu.PrefetchScalarGridSpec(
            num_scalar_prefetch=1,
            grid=(1,),
            in_specs=[pl.BlockSpec(part.shape, lambda n, place: (0, 0, 0)) for part in parts],
            out_specs=[pl.BlockSpec((spread, tokens, rows_in), lambda n, place: (0, 0, 0))] * pieces,
            scratch_shapes=[pltpu.VMEM((2 * len(parts), tokens, rows_in), jnp.bfloat16)],
        ),
        out_shape=[jax.ShapeDtypeStruct((spread, tokens, rows_in), jnp.bfloat16)] * pieces,
        compiler_params=pltpu.CompilerParams(vmem_limit_bytes=24 * MIB),
        cost_estimate=pl.CostEstimate(flops=0, bytes_accessed=4 * pieces * spread * tokens * rows_in, transcendentals=0),
        name="sort_home",
    )(place, *parts)


def assemble_body(count, sizes, place_ref, *refs):
    part_refs, out_ref = refs[:count], refs[count]
    me = place_ref[place_ref.shape[0] - 1]
    spread, _, rows_in = part_refs[0].shape
    begin = at = 0
    for whole in sizes:
        size = whole // count
        for d, ref in enumerate(part_refs):
            rows = pl.ds(pl.multiple_of(begin + (me ^ d) * size, 16), size)
            for n in range(spread):
                out_ref[rows, n * rows_in:(n + 1) * rows_in] = ref[n, at:at + size, :]
        begin += whole
        at += size


def assemble(place, parts, sizes):
    spread, tokens, rows_in = parts[0].shape
    return pl.pallas_call(
        functools.partial(assemble_body, len(parts), sizes),
        grid_spec=pltpu.PrefetchScalarGridSpec(
            num_scalar_prefetch=1,
            grid=(1,),
            in_specs=[pl.BlockSpec(part.shape, lambda n, place: (0, 0, 0)) for part in parts],
            out_specs=pl.BlockSpec((sum(sizes), spread * rows_in), lambda n, place: (0, 0)),
        ),
        out_shape=jax.ShapeDtypeStruct((sum(sizes), spread * rows_in), jnp.bfloat16),
        compiler_params=pltpu.CompilerParams(vmem_limit_bytes=24 * MIB),
        cost_estimate=pl.CostEstimate(
            flops=0, bytes_accessed=4 * len(parts) * spread * tokens * rows_in, transcendentals=0
        ),
        name="assemble",
    )(place, *parts)


def ring_order(chips):
    return [0] + list(range(1, chips, 2)) + list(range(chips - 2 + chips % 2, 0, -2))


def local(layer_input, attn_grad, queries, keys, values, masked, key_bias, w_query, w_key, w_value):
    row_count = lax.axis_size("row")
    col_count = lax.axis_size("col")
    length, width = queries.shape[1], queries.shape[2]
    rows_in = w_query.shape[0]
    spread = row_count // col_count
    chips = row_count // 2
    sizes = chunk_sizes(length)
    weights = (w_query, w_key, w_value)

    order = ring_order(chips)
    ring = [(2 * order[n] + core, 2 * order[(n + 1) % chips] + core) for n in range(chips) for core in range(2)]
    swap = [(n, n ^ 1) for n in range(row_count)]
    table = []
    for row in range(row_count):
        for col in range(col_count):
            at, core = order.index(row // 2), row % 2
            origin = [2 * order[(at - step) % chips] + (core ^ which) for step in range(chips) for which in range(2)]
            slot = [2 * ((order.index(r // 2) - at) % chips) + (r % 2 ^ core) for r in range(row_count)]
            slot = [slot[(col ^ d) * spread + n] for d in range(col_count) for n in range(spread)]
            table.append(origin + slot + [col])
    my_col = lax.axis_index("col")
    place = jnp.array(table, jnp.int32)[lax.axis_index("row") * col_count + my_col]

    def a2a(array, axis):
        return lax.all_to_all(array, axis, split_axis=0, concat_axis=0, tiled=True)

    def after(array, ahead):
        return lax.optimization_barrier((array, ahead))[0]

    always = jnp.sum(masked) >= 0

    def window(work, *operands):
        shapes = jax.eval_shape(work, *operands)

        def nothing(*_):
            return jax.tree.map(lambda leaf: jnp.zeros(leaf.shape, leaf.dtype), shapes)

        return lax.cond(always, work, nothing, *operands)

    every = range(len(sizes))
    last, final = len(sizes) - 1, chips - 1

    def hop(mine):
        return lax.ppermute(mine, "row", ring)

    def other(mine):
        return lax.ppermute(mine, "row", swap)

    def across(mine, apart):
        return lax.ppermute(mine, "col", [(n, n ^ apart) for n in range(col_count)])

    def partial_of(given, ahead=None):
        ahead = given[-1][1] if ahead is None else ahead
        return input_grad(place, [member for pair in given for member in pair], weights, col_count, ahead)

    def summed(partial, beside=()):
        parts = after([across(partial[d], d) if d else partial[d] for d in range(col_count)], beside)
        return sum(part.astype(jnp.float32) for part in parts).astype(jnp.bfloat16)

    def shared(total, chunks_in):
        mine, theirs = [], []
        at = 0
        for size in chunks_in:
            size = size // col_count
            mine.append(total[at:at + size])
            theirs.append(total[at + size:at + 2 * size])
            at += 2 * size
        return jnp.stack([jnp.concatenate(mine, axis=0), other(jnp.concatenate(theirs, axis=0))])

    def weight_part(x, units, given, acc):
        places = [(step, core, index) for step, index in units for core in range(2)]
        return weight_grad(place, x, places, [member for pair in given for member in pair], acc)

    chunks, bias_part = attention(queries[0], keys[0], values[0], attn_grad, masked, key_bias, sizes)
    arrived = [list(chunks)] + [[None] * len(sizes) for _ in range(final)]
    others = [[None] * len(sizes) for _ in range(chips)]
    sums = [None] * chips

    def both(step, index):
        return (arrived[step][index], others[step][index])

    def own_tokens(layer_input, *chunks):
        blocks = layer_input.reshape(length, spread, col_count, rows_in // col_count)
        x = a2a(jnp.transpose(blocks, (2, 1, 0, 3)), "col").reshape(row_count, length, rows_in // col_count)
        theirs = [other(chunk) for chunk in chunks]
        partial = partial_of(list(zip(chunks, theirs)))
        x = a2a(after(x, partial[0]), "row")
        return theirs, shared(summed(partial), sizes), x

    arrived[1][0] = hop(chunks[0])
    others[0], sums[0], x = window(own_tokens, layer_input, *chunks)
    arrived[1][last] = hop(after(chunks[last], others[0][0]))
    x_pieces = {0: x}

    weight_grads = None
    for step in range(1, final):
        units = [(place, spot) for place in range(2) for spot in every] if step == 2 else []

        def early(mine, x, done, partial):
            theirs = other(mine)
            if step == 1:
                return theirs, [across(x, apart) for apart in range(1, col_count) if apart & (apart - 1) == 0]
            if step == 2:
                acc = weight_part(x, units, done, None)
                return theirs, shared(summed(partial, acc[0]), sizes), acc
            return theirs, shared(partial, sizes)

        others[step][0], *given = window(early, arrived[step][0], x, [both(*unit) for unit in units], sums[step - 1])
        if step == 1:
            x_pieces.update(zip([apart for apart in range(1, col_count) if apart & (apart - 1) == 0], given[0]))
        elif step == 2:
            sums[1], weight_grads = given
        else:
            (sums[step - 1],) = given
        arrived[step + 1][0] = hop(after(arrived[step][0], others[step][0]))

        def late(mine, x, sooner, acc):
            theirs = other(mine)
            given = [sooner, (mine, theirs)]
            partial = partial_of(given)
            if step == 1:
                return theirs, partial, [across(x, apart) for apart in range(1, col_count) if apart & (apart - 1)]
            acc = weight_part(x, [(step, spot) for spot in every], given, acc)
            return theirs, summed(partial, acc[0]), acc

        others[step][last], sums[step], given = window(late, arrived[step][last], x, both(step, 0), weight_grads)
        if step == 1:
            x_pieces.update(zip([apart for apart in range(1, col_count) if apart & (apart - 1)], given))
            x = [x_pieces[apart] for apart in range(col_count)]
        else:
            weight_grads = given
        arrived[step + 1][last] = hop(after(arrived[step][last], others[step][last]))

    def before_last(mine, x, acc, total):
        theirs = other(mine)
        given = [(mine, theirs)]
        partial = partial_of(given)
        acc = weight_part(x, [(final, 0)], given, acc)
        return theirs, shared(summed(partial, acc[0]), sizes[:last]), acc, shared(total, sizes)

    others[final][0], sooner, weight_grads, sums[final - 1] = window(
        before_last, after(arrived[final][0], others[final - 1][last]), x, weight_grads, sums[final - 1]
    )

    def homeward(mine, step):
        route = [(2 * order[n] + core, 2 * order[(n - step) % chips] + core) for n in range(chips) for core in range(2)]
        return lax.ppermute(mine, "row", route) if step else mine

    landed = after(arrived[final][last], others[final][0])
    others[final][last] = other(landed)
    sums, sooner = after((sums, sooner), landed)
    at_home = [homeward(sums[step], step) for step in range(final)]
    partial = partial_of([(landed, others[final][last])], others[final][0])

    def folded(bias, bit, ahead):
        bias = after(bias, ahead)
        return bias + lax.ppermute(bias, "row", [(n, n ^ 1 << bit) for n in range(row_count)])

    bias_grad = folded(bias_part, 0, landed)
    total = summed(partial, (at_home, bias_grad))
    sooner = homeward(jnp.concatenate([sooner, shared(total, sizes[last:])], axis=1), final)
    for bit in range(1, row_count.bit_length() - 1):
        bias_grad = folded(bias_grad, bit, total)
    at_home.append(after(sooner, bias_grad))
    mine = sort_home(place, at_home, col_count, spread)
    got = [across(mine[d], d) if d else mine[d] for d in range(col_count)]
    weight_grads = weight_part(after(x, mine), [(final, last)], [both(final, last)], weight_grads)
    layer_grad = assemble(place, after(got, weight_grads[0]), sizes)
    return (layer_grad, *weight_grads, bias_grad)


def solution(mesh):
    in_specs = (
        P("row", "col"),
        P("row", "col"),
        P("row", None, "col"),
        P("row", None, "col"),
        P("row", None, "col"),
        P("row", None),
        P("col"),
        P("row", "col"),
        P("row", "col"),
        P("row", "col"),
    )
    out_specs = (P("row", "col"), P("row", "col"), P("row", "col"), P("row", "col"), P("col"))
    return jax.shard_map(local, mesh=mesh, in_specs=in_specs, out_specs=out_specs, check_vma=False)
```
